512 devices in a mesh: lon: 32 (over x_hi, z), lat: 16 (over y, x_lo, core).
Axes of the slice: x: 4 (x_hi: 2, x_lo: 2; x = x_hi * 2 + x_lo), y: 4, z: 16, core: 2. Of those that a mesh axis runs over, the one named last changes fastest.
Arguments:
- ensemble: bfloat16 [64, 1024, 4096], P(None, 'lat', 'lon'), may hold values from -6 to 6
- right_side: float32 [1024, 4096], P('lat', 'lon'), may hold values from -40 to 40
- obs_error: float32 [1024, 4096], P('lat', 'lon'), may hold values from 0.3 to 3
- valid: int32 [1024, 4096], P('lat', 'lon'), may hold values 0 or 1
- halfwidth: int32 [2], replicated, may hold values from 16 to 32, as said below
Outputs:
- weights: float32 [1024, 4096], P('lat', 'lon')
- residual: float32 [1024, 4096], P('lat', 'lon')
The draws below stay inside these ranges and needn't reach their ends.
Inputs may be any that keep to these rules, and one draw needn't show every extreme that they name: `halfwidth`: one of the two half-widths equals 32 in every draw.
All inputs are finite; a program needn't handle non-finite values. No bound on the sum of `valid` on one device may be relied on, other than what follows from the above.
Results may differ from the reference program's by a relative error of at most 0.024.
Values may be sent and summed in bfloat16 or wider, within the bound.
No kernel may reach another device: no remote copies, remote signals or barrier semaphores. Data moves between devices by JAX's collectives and lax.ppermute only.
A program may use at most 64 MiB of HBM per device.

```python
import math
import jax
import jax.numpy as jnp
from jax import lax

MEMBERS = 64
HMAX = 32
ITERS = 3
NLAT = 1024
NLON = 4096


def draw_halfwidth(key, part):
    key = jax.random.fold_in(key, 11)
    first, second = jax.random.split(key)
    which = jax.random.randint(first, (), 0, 2)
    other = jax.random.randint(second, (), HMAX // 2, HMAX + 1)
    return jnp.where(which == 0, jnp.stack([HMAX + 0 * other, other]), jnp.stack([other, HMAX + 0 * other])).astype(jnp.int32)


def draw_right_side(key, part):
    key = jax.random.fold_in(key, 23)
    along_lat = (jnp.arange(NLAT, dtype=jnp.float32) / NLAT)[:, None]
    along_lon = (jnp.arange(NLON, dtype=jnp.float32) / NLON)[None, :]
    rising = jnp.exp(jnp.log(3.0) * (along_lat + along_lon))
    noise = jnp.clip(jax.random.normal(key, (NLAT, NLON), jnp.float32), -4.0, 4.0)
    return (noise * rising).astype(jnp.float32)


def set_ends(drawn, key, smallest, high):
    place = [jax.random.randint(jax.random.fold_in(key, axis), (), 0, length) for axis, length in enumerate(drawn.shape)]
    main_axis = drawn.shape.index(max(drawn.shape))
    next_to = place[:main_axis] + [(place[main_axis] + 1) % drawn.shape[main_axis]] + place[main_axis + 1:]
    return drawn.at[tuple(place)].set(smallest).at[tuple(next_to)].set(high)


def block_scale(stream_key, extent, cuts, smallest, high):
    def one(dim, blocks):
        steps = jax.random.uniform(jax.random.fold_in(jax.random.fold_in(stream_key, 6), dim), (blocks,), jnp.float32, smallest / len(cuts), high / len(cuts))
        return jnp.repeat(jnp.exp(steps), extent[dim] // blocks).reshape((-1,) + (1,) * (len(extent) - dim - 1))

    level = one(*cuts[0])
    for cut in cuts[1:]:
        level = level * one(*cut)
    return level


def normal_values(key, shape, scale, limit, cuts=(), kind=jnp.bfloat16):
    entries = jax.random.normal(key, shape, jnp.float32) * scale
    if len(cuts) > 0:
        entries = block_scale(key, shape, cuts, -0.22, 0.18) * entries
    return jnp.clip(entries, min=-limit, max=limit).astype(kind)


def setup_inputs(seed: int = 0) -> dict:
    arg_keys = jax.random.split(jax.random.key(seed), 6)
    return {
        "ensemble": normal_values(arg_keys[0], (MEMBERS, NLAT, NLON), 1.0, 6.0, ((1, 16), (2, 32))),
        "right_side": draw_right_side(jax.random.fold_in(arg_keys[5], 71), 0),
        "obs_error": jnp.clip(jnp.exp(math.log(3.0) - 2.3025851 * jax.random.uniform(arg_keys[2], (NLAT, NLON), jnp.float32) ** block_scale(arg_keys[2], (NLAT, NLON), ((0, 16), (1, 32)), -0.2, 0.2)), 0.3, 3.0),
        "valid": set_ends((jax.random.randint(arg_keys[3], (NLAT, NLON), 0, 8) < 7).astype(jnp.int32), jax.random.fold_in(arg_keys[3], 1), 0, 1),
        "halfwidth": draw_halfwidth(jax.random.fold_in(arg_keys[5], 71), 0),
    }


def taper_band(half, width, pad):
    rows = jnp.arange(width + 2 * pad)[:, None]
    cols = jnp.arange(width)[None, :]
    offset = (rows - cols - pad).astype(jnp.float32)
    scale = half.astype(jnp.float32)
    ratio = offset / scale
    return jnp.where(jnp.abs(offset) <= scale, jnp.exp(-4.5 * ratio * ratio), 0.0).astype(jnp.bfloat16)


def lon_taper(field, band, block):
    extended = jnp.concatenate([field[:, NLON - HMAX:], field, field[:, :HMAX]], axis=1)
    starts = (jnp.arange(NLON // block) * block).astype(jnp.int32)
    index = (starts[:, None] + jnp.arange(block + 2 * HMAX)[None, :]).astype(jnp.int32)
    pieces = extended[:, index]
    out = jnp.einsum("abi,ij->abj", pieces.astype(jnp.float32), band.astype(jnp.float32))
    return out.reshape(NLAT, NLON)


def lat_taper(field, band, block):
    extended = jnp.pad(field, ((HMAX, HMAX), (0, 0)))
    starts = (jnp.arange(NLAT // block) * block).astype(jnp.int32)
    index = (starts[:, None] + jnp.arange(block + 2 * HMAX)[None, :]).astype(jnp.int32)
    pieces = extended[index]
    out = jnp.einsum("bin,ia->ban", pieces.astype(jnp.float32), band.astype(jnp.float32))
    return out.reshape(NLAT, NLON)


def reference(ensemble, right_side, obs_error, valid, halfwidth):
    block = 2 * HMAX
    band_lon = taper_band(halfwidth[0], block, HMAX)
    band_lat = taper_band(halfwidth[1], block, HMAX)
    maskf = valid.astype(jnp.float32)

    def operate(vector):
        masked = maskf * vector

        def member(total, anomaly):
            product = (anomaly * masked).astype(jnp.bfloat16)
            first = lon_taper(product, band_lon, block).astype(jnp.bfloat16)
            second = lat_taper(first, band_lat, block)
            return total + anomaly.astype(jnp.float32) * second, None

        total, _ = lax.scan(member, jnp.zeros((NLAT, NLON), jnp.float32), ensemble)
        return maskf * total / (MEMBERS - 1) + obs_error * vector

    weights = jnp.zeros_like(right_side)
    residual, direction = right_side, right_side
    norm_now = jnp.sum(residual * residual)
    for step in range(ITERS):
        image = operate(direction)
        alpha = norm_now / jnp.sum(direction * image)
        weights = weights + alpha * direction
        residual = residual - alpha * image
        norm_next = jnp.sum(residual * residual)
        direction = residual + (norm_next / norm_now) * direction
        norm_now = norm_next
    return weights, residual
```

```python
import functools

import jax
import jax.numpy as jnp
from jax import lax
from jax.experimental import pallas as pl
from jax.experimental.pallas import tpu as pltpu
from jax.sharding import PartitionSpec as P

HMAX = 32
BLOCKS = 4
VMEM_LIMIT = 40 * 1024 * 1024


def shift(cells, axis, step, closed):
    count = lax.axis_size(axis)
    pairs = [(i, (i + step) % count) for i in range(count) if closed or 0 <= i + step < count]
    return lax.ppermute(cells, axis, pairs)


def taper_weight(offset, half):
    offset = offset.astype(jnp.float32)
    scale = half.astype(jnp.float32)
    ratio = offset / scale
    return jnp.where(jnp.abs(offset) <= scale, jnp.exp(-4.5 * ratio * ratio), 0.0).astype(
        jnp.bfloat16
    )


def lon_bands(half, cols):
    lane = jnp.arange(cols)
    strip = jnp.where(lane % 64 < 32, lane % 64 - 32, cols + lane % 64 - 32)
    source = jnp.concatenate([lane, strip])
    offset = source[:, None] - lane[None, :]
    weight = taper_weight(offset, half)
    member = jnp.concatenate([jnp.full((cols,), -1), lane // 64])
    pair = jnp.arange(2)
    keep = (member[None, :] == -1) | (member[None, :] == pair[:, None])
    return jnp.where(keep[:, :, None], weight[None], jnp.zeros((), jnp.bfloat16))


def lat_band(half, rows):
    row = jnp.arange(rows)
    halo = jnp.arange(HMAX)
    source = jnp.concatenate([row, halo - HMAX, rows + halo])
    return taper_weight(source[None, :] - row[:, None], half)


def split3(x):
    hi = x.astype(jnp.bfloat16)
    rest = x - hi.astype(jnp.float32)
    mid = rest.astype(jnp.bfloat16)
    low = (rest - mid.astype(jnp.float32)).astype(jnp.bfloat16)
    return hi, mid, low


def join3(ref, first):
    parts = [ref[first + k].astype(jnp.float32) for k in range(3)]
    return parts[0] + parts[1] + parts[2]


def lanes(shape):
    return lax.broadcasted_iota(jnp.int32, shape, len(shape) - 1)


def edge_tiles(q):
    lane = lanes(q.shape)
    right = jnp.where(lane >= 96, q, 0.0)
    right = right + pltpu.roll(right, 64, 1)
    right = right + pltpu.roll(right, 32, 1)
    left = jnp.where(lane < 32, q, 0.0)
    left = left + pltpu.roll(left, 64, 1)
    left = left + pltpu.roll(left, 32, 1)
    return right, left


def pack_kernel(ens, right_side, valid, east, west, south, north):
    members, rows, cols = ens.shape
    source = lax.broadcasted_iota(jnp.int32, (4 * cols, 2 * cols), 0)
    target = lax.broadcasted_iota(jnp.int32, (4 * cols, 2 * cols), 1)
    lane = target % cols
    wanted = (lane // 32) * cols + lane % 32 + jnp.where(target < cols, 96, 0)
    select = jnp.where(source == wanted, 1.0, 0.0).astype(jnp.bfloat16)
    for i in range(members // 4):
        quad = jnp.concatenate([ens[4 * i + g] for g in range(4)], axis=1)
        both = jnp.dot(quad, select, preferred_element_type=jnp.float32).astype(jnp.bfloat16)
        east[i] = both[:, :cols]
        west[i] = both[:, cols:]
    q = valid[...].astype(jnp.float32) * right_side[...]
    right, left = edge_tiles(q)
    for k, part in enumerate(split3(right)):
        east[members // 4 + k] = part
    for k, part in enumerate(split3(left)):
        west[members // 4 + k] = part
    south[0:members] = ens[:, rows - HMAX :, :]
    north[0:members] = ens[:, :HMAX, :]
    for k, part in enumerate(split3(q)):
        south[members + k] = part[rows - HMAX :]
        north[members + k] = part[:HMAX]


def sides_kernel(from_west, from_east, sides, q_sides, south, north):
    planes, rows, cols = sides.shape
    quads = planes // 2
    source = lax.broadcasted_iota(jnp.int32, (2 * cols, 2 * cols), 0)
    target = lax.broadcasted_iota(jnp.int32, (2 * cols, 2 * cols), 1)
    wanted = (target // 64) * 32 + target % 32 + jnp.where(target % 64 < 32, 0, cols)
    select = jnp.where(source == wanted, 1.0, 0.0).astype(jnp.bfloat16)
    for i in range(quads):
        pair = jnp.concatenate([from_west[i], from_east[i]], axis=1)
        both = jnp.dot(pair, select, preferred_element_type=jnp.float32).astype(jnp.bfloat16)
        for k in range(2):
            part = both[:, k * cols : (k + 1) * cols]
            sides[2 * i + k] = part
            south[2 * i + k] = part[rows - HMAX :]
            north[2 * i + k] = part[:HMAX]
    left = lanes((rows, cols)) % 64 < 32
    q = jnp.where(left, join3(from_west, quads), join3(from_east, quads))
    q_sides[...] = q
    for k, part in enumerate(split3(q)):
        south[planes + k] = part[rows - HMAX :]
        north[planes + k] = part[:HMAX]


def merge_kernel(vector, valid, from_west, from_east, q_sides, south, north):
    rows, cols = vector.shape
    q = valid[...].astype(jnp.float32) * vector[...]
    side = jnp.where(lanes((rows, cols)) % 64 < 32, from_west[...], from_east[...])
    q_sides[...] = side
    south[0:HMAX] = q[rows - HMAX :]
    south[HMAX:] = side[rows - HMAX :]
    north[0:HMAX] = q[:HMAX]
    north[HMAX:] = side[:HMAX]


def gram_lanes(vectors):
    lane = lanes((1, 128))
    out = jnp.zeros((1, 128), jnp.float32)
    for k, (i, j) in enumerate(GRAM):
        out = jnp.where(lane == k, jnp.sum(vectors[i] * vectors[j], keepdims=True), out)
    return out


GRAM = [(0, 0), (0, 1), (0, 2), (0, 3), (1, 1), (1, 2), (1, 3), (2, 2), (2, 3)]


def high_low(x):
    high = x.astype(jnp.bfloat16)
    return high, (x - high.astype(jnp.float32)).astype(jnp.bfloat16)


def apply_kernel(
    step, members, vector, valid, obs_error, q_sides, north_q, south_q, ens, sides,
    north, north_sides, south, south_sides, lon_band, lat_weights, *rest,
):
    earlier, (out, east, west), total = rest[: step], rest[step:-1][:3], rest[-1]
    extra = rest[step:-1][3:]
    block = pl.program_id(0)
    rows, cols = vector.shape

    @pl.when(block == 0)
    def _():
        total[...] = jnp.zeros_like(total)

    q = valid[...].astype(jnp.float32) * vector[...]
    if step == 0:
        above, above_sides = join3(north_q, 0), join3(north_q, 3)
        below, below_sides = join3(south_q, 0), join3(south_q, 3)
    else:
        above, above_sides = north_q[:HMAX], north_q[HMAX:]
        below, below_sides = south_q[:HMAX], south_q[HMAX:]
    tall = jnp.concatenate([q, above, below], axis=0)
    tall_sides = jnp.concatenate([q_sides[...], above_sides, below_sides], axis=0)
    lat = lat_weights[...]
    lat2 = jnp.concatenate([lat, lat], axis=1)
    acc = total[...]
    for j in range(sides.shape[0]):
        plane = jnp.concatenate([sides[j], north_sides[j], south_sides[j]], axis=0)
        side_high, side_low = high_low(plane.astype(jnp.float32) * tall_sides)
        for k in range(2):
            m = 2 * j + k
            own = ens[m]
            anomaly = jnp.concatenate([own, north[m], south[m]], axis=0)
            high, low = high_low(anomaly.astype(jnp.float32) * tall)
            band = lon_band[k]
            first = jnp.dot(
                jnp.concatenate([high, side_high], axis=1), band,
                preferred_element_type=jnp.float32,
            ) + jnp.dot(
                jnp.concatenate([low, side_low], axis=1), band,
                preferred_element_type=jnp.float32,
            )
            second = jnp.dot(
                lat2, jnp.concatenate(high_low(first), axis=0),
                preferred_element_type=jnp.float32,
            )
            acc = acc + own.astype(jnp.float32) * second
    total[...] = acc

    @pl.when(block == pl.num_programs(0) - 1)
    def _():
        maskf = valid[...].astype(jnp.float32)
        image = maskf * acc / (members - 1) + obs_error[...] * vector[...]
        out[...] = image
        east[...], west[...] = edge_tiles(maskf * image)
        if step == 2:
            vectors = [ref[...] for ref in earlier] + [vector[...], image]
            extra[0][...] = jnp.broadcast_to(gram_lanes(vectors)[None], extra[0].shape)


def apply(step, members, vector, valid, obs_error, q_sides, north_q, south_q, ens, sides,
          north, north_sides, south, south_sides, lon_band, lat_weights, earlier=(), peers=0):
    rows, cols = vector.shape
    per = members // BLOCKS

    def whole(a):
        return pl.BlockSpec(a.shape, lambda b, n=a.ndim: (0,) * n)

    def part(count, height):
        return pl.BlockSpec((count, height, cols), lambda b: (b, 0, 0))

    field = jax.ShapeDtypeStruct((rows, cols), jnp.float32)
    outs = [field] * 3
    if step == 2:
        outs.append(jax.ShapeDtypeStruct((peers, 1, 128), jnp.float32))
    return pl.pallas_call(
        functools.partial(apply_kernel, step, members),
        grid=(BLOCKS,),
        in_specs=[
            whole(vector), whole(valid), whole(obs_error), whole(q_sides), whole(north_q),
            whole(south_q), part(per, rows), part(per // 2, rows), part(per, HMAX),
            part(per // 2, HMAX), part(per, HMAX), part(per // 2, HMAX), whole(lon_band),
            whole(lat_weights),
        ] + [whole(a) for a in earlier],
        out_specs=[whole(a) for a in outs],
        out_shape=outs,
        scratch_shapes=[pltpu.VMEM((rows, cols), jnp.float32)],
        compiler_params=pltpu.CompilerParams(vmem_limit_bytes=VMEM_LIMIT),
        name=f"apply_{step}",
    )(vector, valid, obs_error, q_sides, north_q, south_q, ens, sides, north, north_sides,
      south, south_sides, lon_band, lat_weights, *earlier)


def sum_kernel(parts, out):
    out[...] = jnp.broadcast_to(jnp.sum(parts[...], axis=0, keepdims=True), out.shape)


def solve_kernel(parts, v0, v1, v2, v3, weights, residual):
    sums = jnp.sum(parts[...], axis=0)
    lane = lanes(sums.shape)
    gram = {}
    for k, (i, j) in enumerate(GRAM):
        value = jnp.sum(jnp.where(lane == k, sums, 0.0), keepdims=True)
        gram[i, j] = gram[j, i] = value

    def inner(a, b):
        total = None
        for i, x in a.items():
            for j, y in b.items():
                term = x * y * gram[i, j]
                total = term if total is None else total + term
        return total

    def combine(a, scale, b):
        out = dict(a)
        for i, y in b.items():
            out[i] = out[i] + scale * y if i in out else scale * y
        return out

    one = jnp.ones((1, 1), jnp.float32)
    w, r, d = {}, {0: one}, {0: one}
    now = inner(r, r)
    for step in range(3):
        image = {i + 1: x for i, x in d.items()}
        alpha = now / inner(d, image)
        w = combine(w, alpha, d)
        r = combine(r, -alpha, image)
        if step < 2:
            later = inner(r, r)
            d = combine(r, later / now, d)
            now = later
    basis = [v0[...], v1[...], v2[...], v3[...]]
    weights[...] = w[0] * basis[0] + w[1] * basis[1] + w[2] * basis[2]
    residual[...] = r[0] * basis[0] + r[1] * basis[1] + r[2] * basis[2] + r[3] * basis[3]


def call(kernel, outs, *args):
    return pl.pallas_call(
        kernel,
        out_shape=outs,
        compiler_params=pltpu.CompilerParams(vmem_limit_bytes=VMEM_LIMIT),
        name=kernel.__name__,
    )(*args)


def shards(ensemble, right_side, obs_error, valid, halfwidth):
    members, rows, cols = ensemble.shape
    quads, planes = members // 4, members // 2
    bf16 = functools.partial(jax.ShapeDtypeStruct, dtype=jnp.bfloat16)
    f32 = functools.partial(jax.ShapeDtypeStruct, dtype=jnp.float32)
    lon_band = lon_bands(halfwidth[0], cols)
    lat_weights = lat_band(halfwidth[1], rows)

    east, west, south, north = call(
        pack_kernel,
        [bf16((quads + 3, rows, cols))] * 2 + [bf16((members + 3, HMAX, cols))] * 2,
        ensemble, right_side, valid,
    )
    from_west = shift(east, "lon", 1, True)
    from_east = shift(west, "lon", -1, True)
    from_north = shift(south, "lat", 1, False)
    from_south = shift(north, "lat", -1, False)
    sides, q_sides, south, north = call(
        sides_kernel,
        [bf16((planes, rows, cols)), f32((rows, cols))] + [bf16((planes + 3, HMAX, cols))] * 2,
        from_west, from_east,
    )
    north_sides = shift(south, "lat", 1, False)
    south_sides = shift(north, "lat", -1, False)
    north_q = jnp.concatenate([from_north[members:], north_sides[planes:]])
    south_q = jnp.concatenate([from_south[members:], south_sides[planes:]])

    vectors = [right_side]
    for step in range(3):
        out = apply(
            step, members, vectors[-1], valid, obs_error, q_sides, north_q, south_q, ensemble,
            sides, from_north, north_sides, from_south, south_sides, lon_band, lat_weights,
            vectors[:step], lax.axis_size("lat"),
        )
        vectors.append(out[0])
        if step < 2:
            left = shift(out[1], "lon", 1, True)
            right = shift(out[2], "lon", -1, True)
            q_sides, south, north = call(
                merge_kernel, [f32((rows, cols))] + [f32((2 * HMAX, cols))] * 2,
                out[0], valid, left, right,
            )
            north_q = shift(south, "lat", 1, False)
            south_q = shift(north, "lat", -1, False)
    parts = lax.all_to_all(out[3], "lat", 0, 0)
    parts = call(sum_kernel, f32((lax.axis_size("lon"), 1, 128)), parts)
    parts = lax.all_to_all(parts, "lon", 0, 0)
    return tuple(call(solve_kernel, [f32((rows, cols))] * 2, parts, *vectors))


def solution(mesh):
    in_specs = (P(None, "lat", "lon"), P("lat", "lon"), P("lat", "lon"), P("lat", "lon"), P())
    out_specs = (P("lat", "lon"), P("lat", "lon"))
    return jax.shard_map(shards, mesh=mesh, in_specs=in_specs, out_specs=out_specs, check_vma=False)
```

```python
import functools

import jax
import jax.numpy as jnp
from jax import lax
from jax.experimental import pallas as pl
from jax.experimental.pallas import tpu as pltpu
from jax.sharding import PartitionSpec as P

HMAX = 32
BLOCKS = 1
VMEM_LIMIT = 40 * 1024 * 1024


def shift(cells, axis, step, closed):
    count = lax.axis_size(axis)
    pairs = [(i, (i + step) % count) for i in range(count) if closed or 0 <= i + step < count]
    return lax.ppermute(cells, axis, pairs)


def taper_weight(offset, half):
    offset = offset.astype(jnp.float32)
    scale = half.astype(jnp.float32)
    ratio = offset / scale
    return jnp.where(jnp.abs(offset) <= scale, jnp.exp(-4.5 * ratio * ratio), 0.0).astype(
        jnp.bfloat16
    )


def lon_bands(half, cols):
    lane = jnp.arange(cols)
    strip = jnp.where(lane % 64 < 32, lane % 64 - 32, cols + lane % 64 - 32)
    source = jnp.concatenate([lane, strip])
    offset = source[:, None] - lane[None, :]
    weight = taper_weight(offset, half)
    member = jnp.concatenate([jnp.full((cols,), -1), lane // 64])
    pair = jnp.arange(2)
    keep = (member[None, :] == -1) | (member[None, :] == pair[:, None])
    return jnp.where(keep[:, :, None], weight[None], jnp.zeros((), jnp.bfloat16))


def lat_band(half, rows):
    row = jnp.arange(rows)
    halo = jnp.arange(HMAX)
    source = jnp.concatenate([row, halo - HMAX, rows + halo])
    return taper_weight(source[None, :] - row[:, None], half)


def split3(x):
    hi = x.astype(jnp.bfloat16)
    rest = x - hi.astype(jnp.float32)
    mid = rest.astype(jnp.bfloat16)
    low = (rest - mid.astype(jnp.float32)).astype(jnp.bfloat16)
    return hi, mid, low


def join3(ref, first):
    parts = [ref[first + k].astype(jnp.float32) for k in range(3)]
    return parts[0] + parts[1] + parts[2]


def lanes(shape):
    return lax.broadcasted_iota(jnp.int32, shape, len(shape) - 1)


def edge_tiles(q):
    lane = lanes(q.shape)
    right = jnp.where(lane >= 96, q, 0.0)
    right = right + pltpu.roll(right, 64, 1)
    right = right + pltpu.roll(right, 32, 1)
    left = jnp.where(lane < 32, q, 0.0)
    left = left + pltpu.roll(left, 64, 1)
    left = left + pltpu.roll(left, 32, 1)
    return right, left


def pack_kernel(ens, right_side, valid, east, west, south, north):
    members, rows, cols = ens.shape
    source = lax.broadcasted_iota(jnp.int32, (4 * cols, 2 * cols), 0)
    target = lax.broadcasted_iota(jnp.int32, (4 * cols, 2 * cols), 1)
    lane = target % cols
    wanted = (lane // 32) * cols + lane % 32 + jnp.where(target < cols, 96, 0)
    select = jnp.where(source == wanted, 1.0, 0.0).astype(jnp.bfloat16)
    for i in range(members // 4):
        quad = jnp.concatenate([ens[4 * i + g] for g in range(4)], axis=1)
        both = jnp.dot(quad, select, preferred_element_type=jnp.float32).astype(jnp.bfloat16)
        east[i] = both[:, :cols]
        west[i] = both[:, cols:]
    q = valid[...].astype(jnp.float32) * right_side[...]
    right, left = edge_tiles(q)
    for k, part in enumerate(split3(right)):
        east[members // 4 + k] = part
    for k, part in enumerate(split3(left)):
        west[members // 4 + k] = part
    south[0:members] = ens[:, rows - HMAX :, :]
    north[0:members] = ens[:, :HMAX, :]
    for k, part in enumerate(split3(q)):
        south[members + k] = part[rows - HMAX :]
        north[members + k] = part[:HMAX]


def sides_kernel(from_west, from_east, sides, q_sides, south, north):
    planes, rows, cols = sides.shape
    quads = planes // 2
    source = lax.broadcasted_iota(jnp.int32, (2 * cols, 2 * cols), 0)
    target = lax.broadcasted_iota(jnp.int32, (2 * cols, 2 * cols), 1)
    wanted = (target // 64) * 32 + target % 32 + jnp.where(target % 64 < 32, 0, cols)
    select = jnp.where(source == wanted, 1.0, 0.0).astype(jnp.bfloat16)
    for i in range(quads):
        pair = jnp.concatenate([from_west[i], from_east[i]], axis=1)
        both = jnp.dot(pair, select, preferred_element_type=jnp.float32).astype(jnp.bfloat16)
        for k in range(2):
            part = both[:, k * cols : (k + 1) * cols]
            sides[2 * i + k] = part
            south[2 * i + k] = part[rows - HMAX :]
            north[2 * i + k] = part[:HMAX]
    left = lanes((rows, cols)) % 64 < 32
    q = jnp.where(left, join3(from_west, quads), join3(from_east, quads))
    q_sides[...] = q
    for k, part in enumerate(split3(q)):
        south[planes + k] = part[rows - HMAX :]
        north[planes + k] = part[:HMAX]


def merge_kernel(vector, valid, from_west, from_east, q_sides, south, north):
    rows, cols = vector.shape
    q = valid[...].astype(jnp.float32) * vector[...]
    side = jnp.where(lanes((rows, cols)) % 64 < 32, from_west[...], from_east[...])
    q_sides[...] = side
    south[0:HMAX] = q[rows - HMAX :]
    south[HMAX:] = side[rows - HMAX :]
    north[0:HMAX] = q[:HMAX]
    north[HMAX:] = side[:HMAX]


def gram_lanes(vectors):
    lane = lanes((1, 128))
    out = jnp.zeros((1, 128), jnp.float32)
    for k, (i, j) in enumerate(GRAM):
        out = jnp.where(lane == k, jnp.sum(vectors[i] * vectors[j], keepdims=True), out)
    return out


GRAM = [(0, 0), (0, 1), (0, 2), (0, 3), (1, 1), (1, 2), (1, 3), (2, 2), (2, 3)]


def high_low(x):
    high = x.astype(jnp.bfloat16)
    return high, (x - high.astype(jnp.float32)).astype(jnp.bfloat16)


def apply_kernel(
    step, members, vector, valid, obs_error, q_sides, north_q, south_q, ens, sides,
    north, north_sides, south, south_sides, lon_band, lat_weights, *rest,
):
    earlier, (out, east, west), total = rest[: step], rest[step:-1][:3], rest[-1]
    extra = rest[step:-1][3:]
    block = pl.program_id(0)
    rows, cols = vector.shape

    @pl.when(block == 0)
    def _():
        total[...] = jnp.zeros_like(total)

    q = valid[...].astype(jnp.float32) * vector[...]
    if step == 0:
        above, above_sides = join3(north_q, 0), join3(north_q, 3)
        below, below_sides = join3(south_q, 0), join3(south_q, 3)
    else:
        above, above_sides = north_q[:HMAX], north_q[HMAX:]
        below, below_sides = south_q[:HMAX], south_q[HMAX:]
    tall = jnp.concatenate([q, above, below], axis=0)
    tall_sides = jnp.concatenate([q_sides[...], above_sides, below_sides], axis=0)
    lat = lat_weights[...]
    lat2 = jnp.concatenate([lat, lat], axis=1)
    acc = total[...]
    n = sides.shape[0]
    own_band = lon_band[0][:cols]
    own_band2 = jnp.concatenate([own_band, own_band], axis=0)
    side_band = jnp.concatenate([lon_band[0][cols:], lon_band[1][cols:]], axis=1)
    side_band2 = jnp.concatenate([side_band, side_band], axis=0)
    lo_list, hi_list = [], []
    for j in range(n):
        plane = jnp.concatenate([sides[j], north_sides[j], south_sides[j]], axis=0)
        hi_list.append(jnp.concatenate(high_low(plane.astype(jnp.float32) * tall_sides), axis=1))
    side = jnp.dot(jnp.concatenate(hi_list, axis=0), side_band2, preferred_element_type=jnp.float32)
    for m in range(2 * n):
        anomaly = jnp.concatenate([ens[m], north[m], south[m]], axis=0)
        lo_list.append(jnp.concatenate(high_low(anomaly.astype(jnp.float32) * tall), axis=1))
    main = jnp.dot(jnp.concatenate(lo_list, axis=0), own_band2, preferred_element_type=jnp.float32)
    for j in range(n):
        cs = []
        for k in range(2):
            m = 2 * j + k
            first = main[128 * m : 128 * m + 128] + side[128 * j : 128 * j + 128, 128 * k : 128 * k + 128]
            cs.append(jnp.concatenate(high_low(first), axis=0))
        second = jnp.dot(lat2, jnp.concatenate(cs, axis=1), preferred_element_type=jnp.float32)
        for k in range(2):
            acc = acc + ens[2 * j + k].astype(jnp.float32) * second[:, 128 * k : 128 * k + 128]
    total[...] = acc

    @pl.when(block == pl.num_programs(0) - 1)
    def _():
        maskf = valid[...].astype(jnp.float32)
        image = maskf * acc / (members - 1) + obs_error[...] * vector[...]
        out[...] = image
        east[...], west[...] = edge_tiles(maskf * image)
        if step == 2:
            vectors = [ref[...] for ref in earlier] + [vector[...], image]
            extra[0][...] = jnp.broadcast_to(gram_lanes(vectors)[None], extra[0].shape)


def apply(step, members, vector, valid, obs_error, q_sides, north_q, south_q, ens, sides,
          north, north_sides, south, south_sides, lon_band, lat_weights, earlier=(), peers=0):
    rows, cols = vector.shape
    per = members // BLOCKS

    def whole(a):
        return pl.BlockSpec(a.shape, lambda b, n=a.ndim: (0,) * n)

    def part(count, height):
        return pl.BlockSpec((count, height, cols), lambda b: (b, 0, 0))

    field = jax.ShapeDtypeStruct((rows, cols), jnp.float32)
    outs = [field] * 3
    if step == 2:
        outs.append(jax.ShapeDtypeStruct((peers, 1, 128), jnp.float32))
    return pl.pallas_call(
        functools.partial(apply_kernel, step, members),
        grid=(BLOCKS,),
        in_specs=[
            whole(vector), whole(valid), whole(obs_error), whole(q_sides), whole(north_q),
            whole(south_q), part(per, rows), part(per // 2, rows), part(per, HMAX),
            part(per // 2, HMAX), part(per, HMAX), part(per // 2, HMAX), whole(lon_band),
            whole(lat_weights),
        ] + [whole(a) for a in earlier],
        out_specs=[whole(a) for a in outs],
        out_shape=outs,
        scratch_shapes=[pltpu.VMEM((rows, cols), jnp.float32)],
        compiler_params=pltpu.CompilerParams(vmem_limit_bytes=VMEM_LIMIT),
        name=f"apply_{step}",
    )(vector, valid, obs_error, q_sides, north_q, south_q, ens, sides, north, north_sides,
      south, south_sides, lon_band, lat_weights, *earlier)


def sum_kernel(parts, out):
    out[...] = jnp.broadcast_to(jnp.sum(parts[...], axis=0, keepdims=True), out.shape)


def solve_kernel(parts, v0, v1, v2, v3, weights, residual):
    sums = jnp.sum(parts[...], axis=0)
    lane = lanes(sums.shape)
    gram = {}
    for k, (i, j) in enumerate(GRAM):
        value = jnp.sum(jnp.where(lane == k, sums, 0.0), keepdims=True)
        gram[i, j] = gram[j, i] = value

    def inner(a, b):
        total = None
        for i, x in a.items():
            for j, y in b.items():
                term = x * y * gram[i, j]
                total = term if total is None else total + term
        return total

    def combine(a, scale, b):
        out = dict(a)
        for i, y in b.items():
            out[i] = out[i] + scale * y if i in out else scale * y
        return out

    one = jnp.ones((1, 1), jnp.float32)
    w, r, d = {}, {0: one}, {0: one}
    now = inner(r, r)
    for step in range(3):
        image = {i + 1: x for i, x in d.items()}
        alpha = now / inner(d, image)
        w = combine(w, alpha, d)
        r = combine(r, -alpha, image)
        if step < 2:
            later = inner(r, r)
            d = combine(r, later / now, d)
            now = later
    basis = [v0[...], v1[...], v2[...], v3[...]]
    weights[...] = w[0] * basis[0] + w[1] * basis[1] + w[2] * basis[2]
    residual[...] = r[0] * basis[0] + r[1] * basis[1] + r[2] * basis[2] + r[3] * basis[3]


def call(kernel, outs, *args):
    return pl.pallas_call(
        kernel,
        out_shape=outs,
        compiler_params=pltpu.CompilerParams(vmem_limit_bytes=VMEM_LIMIT),
        name=kernel.__name__,
    )(*args)


def shards(ensemble, right_side, obs_error, valid, halfwidth):
    members, rows, cols = ensemble.shape
    quads, planes = members // 4, members // 2
    bf16 = functools.partial(jax.ShapeDtypeStruct, dtype=jnp.bfloat16)
    f32 = functools.partial(jax.ShapeDtypeStruct, dtype=jnp.float32)
    lon_band = lon_bands(halfwidth[0], cols)
    lat_weights = lat_band(halfwidth[1], rows)

    east, west, south, north = call(
        pack_kernel,
        [bf16((quads + 3, rows, cols))] * 2 + [bf16((members + 3, HMAX, cols))] * 2,
        ensemble, right_side, valid,
    )
    from_west = shift(east, "lon", 1, True)
    from_east = shift(west, "lon", -1, True)
    from_north = shift(south, "lat", 1, False)
    from_south = shift(north, "lat", -1, False)
    sides, q_sides, south, north = call(
        sides_kernel,
        [bf16((planes, rows, cols)), f32((rows, cols))] + [bf16((planes + 3, HMAX, cols))] * 2,
        from_west, from_east,
    )
    north_sides = shift(south, "lat", 1, False)
    south_sides = shift(north, "lat", -1, False)
    north_q = jnp.concatenate([from_north[members:], north_sides[planes:]])
    south_q = jnp.concatenate([from_south[members:], south_sides[planes:]])

    vectors = [right_side]
    for step in range(3):
        out = apply(
            step, members, vectors[-1], valid, obs_error, q_sides, north_q, south_q, ensemble,
            sides, from_north, north_sides, from_south, south_sides, lon_band, lat_weights,
            vectors[:step], lax.axis_size("lat"),
        )
        vectors.append(out[0])
        if step < 2:
            left = shift(out[1], "lon", 1, True)
            right = shift(out[2], "lon", -1, True)
            q_sides, south, north = call(
                merge_kernel, [f32((rows, cols))] + [f32((2 * HMAX, cols))] * 2,
                out[0], valid, left, right,
            )
            north_q = shift(south, "lat", 1, False)
            south_q = shift(north, "lat", -1, False)
    parts = lax.all_to_all(out[3], "lat", 0, 0)
    parts = call(sum_kernel, f32((lax.axis_size("lon"), 1, 128)), parts)
    parts = lax.all_to_all(parts, "lon", 0, 0)
    return tuple(call(solve_kernel, [f32((rows, cols))] * 2, parts, *vectors))


def solution(mesh):
    in_specs = (P(None, "lat", "lon"), P("lat", "lon"), P("lat", "lon"), P("lat", "lon"), P())
    out_specs = (P("lat", "lon"), P("lat", "lon"))
    return jax.shard_map(shards, mesh=mesh, in_specs=in_specs, out_specs=out_specs, check_vma=False)
```

```python
import functools

import jax
import jax.numpy as jnp
from jax import lax
from jax.experimental import pallas as pl
from jax.experimental.pallas import tpu as pltpu
from jax.sharding import Mesh
from jax.sharding import PartitionSpec as P

HMAX = 32
VMEM_LIMIT = 40 * 1024 * 1024


LON = ("far", "near")


def shift(cells, axis, step, closed):
    count = lax.axis_size(axis)
    pairs = [(i, (i + step) % count) for i in range(count) if closed or 0 <= i + step < count]
    return lax.ppermute(cells, axis, pairs)


def taper_weight(offset, half):
    offset = offset.astype(jnp.float32)
    scale = half.astype(jnp.float32)
    ratio = offset / scale
    return jnp.where(jnp.abs(offset) <= scale, jnp.exp(-4.5 * ratio * ratio), 0.0).astype(
        jnp.bfloat16
    )


def lon_bands(half, cols):
    lane = jnp.arange(cols)
    own = taper_weight(lane[:, None] - lane[None, :], half)
    strip = jnp.where(lane % 64 < 32, lane % 64 - 32, cols + lane % 64 - 32)
    both = jnp.arange(2 * cols)
    weight = taper_weight(strip[:, None] - both[None, :] % cols, half)
    keep = lane[:, None] // 64 == both[None, :] // cols
    side = jnp.where(keep, weight, jnp.zeros((), jnp.bfloat16))
    return jnp.concatenate([own, own]), jnp.concatenate([side, side])


def lat_band(half, rows):
    row = jnp.arange(rows)
    halo = jnp.arange(HMAX)
    target = jnp.concatenate([row, halo - HMAX, rows + halo])
    source = jnp.concatenate([row, row])
    return taper_weight(source[None, :] - target[:, None], half)


def split3(x):
    hi = x.astype(jnp.bfloat16)
    rest = x - hi.astype(jnp.float32)
    mid = rest.astype(jnp.bfloat16)
    low = (rest - mid.astype(jnp.float32)).astype(jnp.bfloat16)
    return hi, mid, low


def join3(ref, first):
    parts = [ref[first + k].astype(jnp.float32) for k in range(3)]
    return parts[0] + parts[1] + parts[2]


def lanes(shape):
    return lax.broadcasted_iota(jnp.int32, shape, len(shape) - 1)


def edge_tiles(q):
    lane = lanes(q.shape)
    right = jnp.where(lane >= 96, q, 0.0)
    right = right + pltpu.roll(right, 64, 1)
    right = right + pltpu.roll(right, 32, 1)
    left = jnp.where(lane < 32, q, 0.0)
    left = left + pltpu.roll(left, 64, 1)
    left = left + pltpu.roll(left, 32, 1)
    return right, left


def pack_kernel(ens, q, valid, east, west, south, north):
    members, rows, cols = ens.shape
    source = lax.broadcasted_iota(jnp.int32, (4 * cols, 2 * cols), 0)
    target = lax.broadcasted_iota(jnp.int32, (4 * cols, 2 * cols), 1)
    lane = target % cols
    wanted = (lane // 32) * cols + lane % 32 + jnp.where(target < cols, 96, 0)
    select = jnp.where(source == wanted, 1.0, 0.0).astype(jnp.bfloat16)
    quads = jnp.concatenate(
        [
            jnp.concatenate([ens[4 * i + g] for g in range(4)], axis=1)
            for i in range(members // 4)
        ],
        axis=0,
    )
    both = jnp.dot(quads, select, preferred_element_type=jnp.float32).astype(jnp.bfloat16)
    for i in range(members // 4):
        east[i] = both[rows * i : rows * (i + 1), :cols]
        west[i] = both[rows * i : rows * (i + 1), cols:]
    right, left = edge_tiles(q[...])
    for k, part in enumerate(split3(right)):
        east[members // 4 + k] = part
    for k, part in enumerate(split3(left)):
        west[members // 4 + k] = part
    mask = valid[...].astype(jnp.float32).astype(jnp.bfloat16)
    south[:members] = ens[:, rows - HMAX :, :]
    south[members] = mask[rows - HMAX :]
    north[:members] = ens[:, :HMAX, :]
    north[members] = mask[:HMAX]


def sides_kernel(from_west, from_east, sides, q_sides):
    planes, rows, cols = sides.shape
    quads = planes // 2
    source = lax.broadcasted_iota(jnp.int32, (2 * cols, 2 * cols), 0)
    target = lax.broadcasted_iota(jnp.int32, (2 * cols, 2 * cols), 1)
    wanted = (target // 64) * 32 + target % 32 + jnp.where(target % 64 < 32, 0, cols)
    select = jnp.where(source == wanted, 1.0, 0.0).astype(jnp.bfloat16)
    pairs = jnp.concatenate(
        [jnp.concatenate([from_west[i], from_east[i]], axis=1) for i in range(quads)], axis=0
    )
    both = jnp.dot(pairs, select, preferred_element_type=jnp.float32).astype(jnp.bfloat16)
    for i in range(quads):
        for k in range(2):
            sides[2 * i + k] = both[rows * i : rows * (i + 1), k * cols : (k + 1) * cols]
    left = lanes((rows, cols)) % 64 < 32
    q_sides[...] = jnp.where(left, join3(from_west, quads), join3(from_east, quads))


def gram_lanes(vectors, last):
    lane = lanes((1, 128))
    out = jnp.where(lane == len(GRAM), last, 0.0)
    for k, (i, j) in enumerate(GRAM):
        out = jnp.where(lane == k, jnp.sum(vectors[i] * vectors[j], keepdims=True), out)
    return out


GRAM = [(0, 0), (0, 1), (0, 2), (1, 1), (1, 2), (2, 2)]


def high_low(x):
    high = x.astype(jnp.bfloat16)
    return high, (x - high.astype(jnp.float32)).astype(jnp.bfloat16)


def taper_kernel(step, vector, valid, obs_error, *refs):
    if step == 0:
        q_sides, refs = refs[0][...], refs[1:]
    else:
        left, right, refs = refs[0], refs[1], refs[2:]
        q_sides = jnp.where(lanes(left.shape) % 64 < 32, left[...], right[...])
    ens, sides, above, below, lon_band, side_band, lat = refs[:7]
    part, up, down = refs[-3:]
    members, rows, cols = ens.shape
    count = members // 2
    maskf = valid[...].astype(jnp.float32)
    q = maskf * vector[...]
    side = jnp.concatenate(
        [
            jnp.concatenate(high_low(sides[j].astype(jnp.float32) * q_sides), axis=1)
            for j in range(count)
        ],
        axis=0,
    )
    side = jnp.dot(side, side_band[...], preferred_element_type=jnp.float32)
    main = jnp.concatenate(
        [
            jnp.concatenate(high_low(ens[m].astype(jnp.float32) * q), axis=1)
            for m in range(members)
        ],
        axis=0,
    )
    main = jnp.dot(main, lon_band[...], preferred_element_type=jnp.float32)
    total = jnp.zeros((rows + 2 * HMAX, cols), jnp.float32)
    for j in range(count):
        first = [
            main[rows * (2 * j + k) : rows * (2 * j + k + 1)]
            + side[rows * j : rows * (j + 1), cols * k : cols * (k + 1)]
            for k in range(2)
        ]
        pair = jnp.concatenate(high_low(jnp.concatenate(first, axis=1)), axis=0)
        second = jnp.dot(lat[...], pair, preferred_element_type=jnp.float32)
        for k in range(2):
            m = 2 * j + k
            there = jnp.concatenate([ens[m], above[m], below[m]], axis=0).astype(jnp.float32)
            total = total + there * second[:, cols * k : cols * (k + 1)]
    total = total / (members - 1)
    image = maskf * total[:rows] + obs_error[...] * vector[...]
    upward, downward = total[rows : rows + HMAX], total[rows + HMAX :]
    part[...] = image
    up[:HMAX] = upward
    down[:HMAX] = downward
    if step == 1:
        up[HMAX:] = image[:HMAX]
        down[HMAX:] = image[rows - HMAX :]


def gram_kernel(v0, v1, v2, part, up, down, q_north, q_south, gram):
    vectors = [v0[...], v1[...], v2[...]]
    around = q_north[...] * up[...] + q_south[...] * down[...]
    last = jnp.sum(vectors[2] * part[...], keepdims=True) + jnp.sum(around, keepdims=True)
    gram[...] = jnp.broadcast_to(gram_lanes(vectors, last)[None], gram.shape)


def whole_image(part, from_north, from_south, valid):
    around = jnp.concatenate([from_north[:HMAX], from_south[:HMAX]], axis=0)
    maskf = valid[...].astype(jnp.float32)
    return part[...] + maskf * around, maskf


def finish_kernel(step, part, from_north, from_south, valid, *refs):
    out, east, west = refs[-5:-2] if step == 1 else refs
    image, maskf = whole_image(part, from_north, from_south, valid)
    out[...] = image
    east[...], west[...] = edge_tiles(maskf * image)
    if step == 1:
        up, down, above, below = refs[:4]
        q_north, q_south = refs[-2:]
        edge = above.shape[0] - 1
        mask_north = above[edge].astype(jnp.float32)
        mask_south = below[edge].astype(jnp.float32)
        q_north[...] = mask_north * (from_north[HMAX:] + mask_north * up[:HMAX])
        q_south[...] = mask_south * (from_south[HMAX:] + mask_south * down[:HMAX])


def sum_kernel(parts, out):
    out[...] = jnp.broadcast_to(jnp.sum(parts[...], axis=0, keepdims=True), out.shape)


def solve_kernel(parts, v0, v1, v2, part, from_north, from_south, valid, weights, residual):
    sums = jnp.sum(parts[...], axis=0)
    lane = lanes(sums.shape)
    gram = {}
    for k, (i, j) in enumerate(GRAM + [(2, 3)]):
        value = jnp.sum(jnp.where(lane == k, sums, 0.0), keepdims=True)
        gram[i, j] = gram[j, i] = value
    gram[0, 3], gram[1, 3] = gram[1, 2], gram[2, 2]

    def inner(a, b):
        total = None
        for i, x in a.items():
            for j, y in b.items():
                term = x * y * gram[i, j]
                total = term if total is None else total + term
        return total

    def combine(a, scale, b):
        out = dict(a)
        for i, y in b.items():
            out[i] = out[i] + scale * y if i in out else scale * y
        return out

    one = jnp.ones((1, 1), jnp.float32)
    w, r, d = {}, {0: one}, {0: one}
    now = inner(r, r)
    for step in range(3):
        image = {i + 1: x for i, x in d.items()}
        alpha = now / inner(d, image)
        w = combine(w, alpha, d)
        r = combine(r, -alpha, image)
        if step < 2:
            later = inner(r, r)
            d = combine(r, later / now, d)
            now = later
    basis = [v0[...], v1[...], v2[...], whole_image(part, from_north, from_south, valid)[0]]
    weights[...] = w[0] * basis[0] + w[1] * basis[1] + w[2] * basis[2]
    residual[...] = r[0] * basis[0] + r[1] * basis[1] + r[2] * basis[2] + r[3] * basis[3]


def call(kernel, outs, *args, name=None, flops=0, **more):
    return pl.pallas_call(
        kernel,
        out_shape=outs,
        compiler_params=pltpu.CompilerParams(vmem_limit_bytes=VMEM_LIMIT),
        cost_estimate=pl.CostEstimate(
            flops=flops, transcendentals=0, bytes_accessed=sum(a.size * a.dtype.itemsize for a in args)
        ),
        name=name or kernel.__name__,
        **more,
    )(*args)


def shards(ensemble, right_side, obs_error, valid, halfwidth):
    members, rows, cols = ensemble.shape
    quads, planes = members // 4, members // 2
    bf16 = functools.partial(jax.ShapeDtypeStruct, dtype=jnp.bfloat16)
    f32 = functools.partial(jax.ShapeDtypeStruct, dtype=jnp.float32)
    lon_band, side_band = lon_bands(halfwidth[0], cols)
    lat = lat_band(halfwidth[1], rows)
    q = valid.astype(jnp.float32) * right_side
    east, west, south, north = call(
        pack_kernel,
        [bf16((quads + 3, rows, cols))] * 2 + [bf16((members + 1, HMAX, cols))] * 2,
        ensemble, q, valid,
    )
    from_west = shift(east, LON, 1, True)
    from_east = shift(west, LON, -1, True)
    above = shift(south, "lat", 1, False)
    below = shift(north, "lat", -1, False)
    sides, q_sides = call(
        sides_kernel, [bf16((planes, rows, cols)), f32((rows, cols))], from_west, from_east
    )
    around = [q_sides]
    vectors, more = [right_side], []
    flops = 8 * members * rows * cols * (cols + rows)
    for step in range(3):
        vector = vectors[-1]
        message = f32((2 * HMAX if step == 1 else HMAX, cols))
        outs = [f32((rows, cols)), message, message]
        part, up, down = call(
            functools.partial(taper_kernel, step), outs,
            vector, valid, obs_error, *around, ensemble, sides, above, below, lon_band,
            side_band, lat, name=f"taper_{step}", flops=flops,
        )
        from_north = shift(down, "lat", 1, False)
        from_south = shift(up, "lat", -1, False)
        if step == 2:
            break
        outs = [f32((rows, cols))] * 3
        if step == 1:
            outs += [f32((HMAX, cols))] * 2
            more = [up, down, above, below]
        image, east, west, *more = call(
            functools.partial(finish_kernel, step), outs, part, from_north, from_south, valid,
            *more, name=f"finish_{step}",
        )
        vectors.append(image)
        around = [shift(east, LON, 1, True), shift(west, LON, -1, True)]
    gram = call(
        gram_kernel, f32((lax.axis_size("far") * lax.axis_size("lat"), 1, 128)),
        *vectors, part, up, down, *more,
    )
    parts = lax.all_to_all(gram, ("far", "lat"), 0, 0)
    parts = call(sum_kernel, f32((lax.axis_size("near"), 1, 128)), parts)
    parts = lax.all_to_all(parts, "near", 0, 0)
    return tuple(
        call(
            solve_kernel, [f32((rows, cols))] * 2, parts, *vectors, part, from_north, from_south,
            valid,
        )
    )


def solution(mesh):
    devices = mesh.devices
    parts = 2 if devices.shape[0] % 2 == 0 else 1
    mesh = Mesh(
        devices.reshape(parts, devices.shape[0] // parts, devices.shape[1]), LON + ("lat",)
    )
    in_specs = (P(None, "lat", LON), P("lat", LON), P("lat", LON), P("lat", LON), P())
    out_specs = (P("lat", LON), P("lat", LON))
    return jax.shard_map(shards, mesh=mesh, in_specs=in_specs, out_specs=out_specs, check_vma=False)
```

```python
import functools

import jax
import jax.numpy as jnp
from jax import lax
from jax.experimental import pallas as pl
from jax.experimental.pallas import tpu as pltpu
from jax.sharding import Mesh
from jax.sharding import PartitionSpec as P

HMAX = 32
VMEM_LIMIT = 40 * 1024 * 1024


LON = ("far", "near")


def shift(cells, axis, step, closed):
    count = lax.axis_size(axis)
    pairs = [(i, (i + step) % count) for i in range(count) if closed or 0 <= i + step < count]
    return lax.ppermute(cells, axis, pairs)


def taper_weight(offset, half):
    offset = offset.astype(jnp.float32)
    scale = half.astype(jnp.float32)
    ratio = offset / scale
    return jnp.where(jnp.abs(offset) <= scale, jnp.exp(-4.5 * ratio * ratio), 0.0).astype(
        jnp.bfloat16
    )


def lon_bands(half, cols):
    lane = jnp.arange(cols)
    own = taper_weight(lane[:, None] - lane[None, :], half)
    strip = jnp.where(lane % 64 < 32, lane % 64 - 32, cols + lane % 64 - 32)
    both = jnp.arange(2 * cols)
    weight = taper_weight(strip[:, None] - both[None, :] % cols, half)
    keep = lane[:, None] // 64 == both[None, :] // cols
    side = jnp.where(keep, weight, jnp.zeros((), jnp.bfloat16))
    return jnp.concatenate([own, own]), jnp.concatenate([side, side])


def lat_band(half, rows):
    row = jnp.arange(rows)
    halo = jnp.arange(HMAX)
    target = jnp.concatenate([row, halo - HMAX, rows + halo])
    source = jnp.concatenate([row, row])
    return taper_weight(source[None, :] - target[:, None], half)


def split3(x):
    hi = x.astype(jnp.bfloat16)
    rest = x - hi.astype(jnp.float32)
    mid = rest.astype(jnp.bfloat16)
    low = (rest - mid.astype(jnp.float32)).astype(jnp.bfloat16)
    return hi, mid, low


def join3(ref, first):
    parts = [ref[first + k].astype(jnp.float32) for k in range(3)]
    return parts[0] + parts[1] + parts[2]


def lanes(shape):
    return lax.broadcasted_iota(jnp.int32, shape, len(shape) - 1)


def edge_tiles(q):
    lane = lanes(q.shape)
    right = jnp.where(lane >= 96, q, 0.0)
    right = right + pltpu.roll(right, 64, 1)
    right = right + pltpu.roll(right, 32, 1)
    left = jnp.where(lane < 32, q, 0.0)
    left = left + pltpu.roll(left, 64, 1)
    left = left + pltpu.roll(left, 32, 1)
    return right, left


def rows_kernel(ens, south, north):
    rows = ens.shape[1]
    south[...] = ens[:, rows - HMAX :, :]
    north[...] = ens[:, :HMAX, :]


def columns_kernel(ens, q, _, __, east, west):
    members, rows, cols = ens.shape
    source = lax.broadcasted_iota(jnp.int32, (4 * cols, 2 * cols), 0)
    target = lax.broadcasted_iota(jnp.int32, (4 * cols, 2 * cols), 1)
    lane = target % cols
    wanted = (lane // 32) * cols + lane % 32 + jnp.where(target < cols, 96, 0)
    select = jnp.where(source == wanted, 1.0, 0.0).astype(jnp.bfloat16)
    quads = jnp.concatenate(
        [
            jnp.concatenate([ens[4 * i + g] for g in range(4)], axis=1)
            for i in range(members // 4)
        ],
        axis=0,
    )
    both = jnp.dot(quads, select, preferred_element_type=jnp.float32).astype(jnp.bfloat16)
    for i in range(members // 4):
        east[i] = both[rows * i : rows * (i + 1), :cols]
        west[i] = both[rows * i : rows * (i + 1), cols:]
    right, left = edge_tiles(q[...])
    for k, part in enumerate(split3(right)):
        east[members // 4 + k] = part
    for k, part in enumerate(split3(left)):
        west[members // 4 + k] = part


def sides_kernel(from_west, from_east, sides, q_sides):
    planes, rows, cols = sides.shape
    quads = planes // 2
    source = lax.broadcasted_iota(jnp.int32, (2 * cols, 2 * cols), 0)
    target = lax.broadcasted_iota(jnp.int32, (2 * cols, 2 * cols), 1)
    wanted = (target // 64) * 32 + target % 32 + jnp.where(target % 64 < 32, 0, cols)
    select = jnp.where(source == wanted, 1.0, 0.0).astype(jnp.bfloat16)
    pairs = jnp.concatenate(
        [jnp.concatenate([from_west[i], from_east[i]], axis=1) for i in range(quads)], axis=0
    )
    both = jnp.dot(pairs, select, preferred_element_type=jnp.float32).astype(jnp.bfloat16)
    for i in range(quads):
        for k in range(2):
            sides[2 * i + k] = both[rows * i : rows * (i + 1), k * cols : (k + 1) * cols]
    left = lanes((rows, cols)) % 64 < 32
    q_sides[...] = jnp.where(left, join3(from_west, quads), join3(from_east, quads))


def gram_lanes(vectors, last):
    lane = lanes((1, 128))
    out = jnp.where(lane == len(GRAM), last, 0.0)
    for k, (i, j) in enumerate(GRAM):
        out = jnp.where(lane == k, jnp.sum(vectors[i] * vectors[j], keepdims=True), out)
    return out


GRAM = [(0, 0), (0, 1), (0, 2), (1, 1), (1, 2), (2, 2)]


def high_low(x):
    high = x.astype(jnp.bfloat16)
    return high, (x - high.astype(jnp.float32)).astype(jnp.bfloat16)


def taper_kernel(step, vector, valid, obs_error, *refs):
    if step == 0:
        q_sides, refs = refs[0][...], refs[1:]
    else:
        left, right, refs = refs[0], refs[1], refs[2:]
        q_sides = jnp.where(lanes(left.shape) % 64 < 32, left[...], right[...])
    ens, sides, above, below, lon_band, side_band, lat = refs[:7]
    part, up, down = refs[-3:]
    members, rows, cols = ens.shape
    count = members // 2
    maskf = valid[...].astype(jnp.float32)
    q = maskf * vector[...]
    side = jnp.concatenate(
        [
            jnp.concatenate(high_low(sides[j].astype(jnp.float32) * q_sides), axis=1)
            for j in range(count)
        ],
        axis=0,
    )
    side = jnp.dot(side, side_band[...], preferred_element_type=jnp.float32)
    main = jnp.concatenate(
        [
            jnp.concatenate(high_low(ens[m].astype(jnp.float32) * q), axis=1)
            for m in range(members)
        ],
        axis=0,
    )
    main = jnp.dot(main, lon_band[...], preferred_element_type=jnp.float32)
    total = jnp.zeros((rows + 2 * HMAX, cols), jnp.float32)
    for j in range(count):
        first = [
            main[rows * (2 * j + k) : rows * (2 * j + k + 1)]
            + side[rows * j : rows * (j + 1), cols * k : cols * (k + 1)]
            for k in range(2)
        ]
        pair = jnp.concatenate(high_low(jnp.concatenate(first, axis=1)), axis=0)
        second = jnp.dot(lat[...], pair, preferred_element_type=jnp.float32)
        for k in range(2):
            m = 2 * j + k
            there = jnp.concatenate([ens[m], above[m], below[m]], axis=0).astype(jnp.float32)
            total = total + there * second[:, cols * k : cols * (k + 1)]
    total = total / (members - 1)
    image = maskf * total[:rows] + obs_error[...] * vector[...]
    upward, downward = total[rows : rows + HMAX], total[rows + HMAX :]
    part[...] = image
    up[:HMAX] = upward
    down[:HMAX] = downward
    if step == 0:
        up[HMAX:] = maskf[:HMAX]
        down[HMAX:] = maskf[rows - HMAX :]
    if step == 1:
        up[HMAX:] = image[:HMAX]
        down[HMAX:] = image[rows - HMAX :]


def gram_kernel(v0, v1, v2, part, up, down, q_north, q_south, gram):
    vectors = [v0[...], v1[...], v2[...]]
    around = q_north[...] * up[...] + q_south[...] * down[...]
    last = jnp.sum(vectors[2] * part[...], keepdims=True) + jnp.sum(around, keepdims=True)
    gram[...] = jnp.broadcast_to(gram_lanes(vectors, last)[None], gram.shape)


def whole_image(part, from_north, from_south, valid):
    around = jnp.concatenate([from_north[:HMAX], from_south[:HMAX]], axis=0)
    maskf = valid[...].astype(jnp.float32)
    return part[...] + maskf * around, maskf


def finish_kernel(step, part, from_north, from_south, valid, *refs):
    out, east, west = refs[-5:-2] if step == 1 else refs
    image, maskf = whole_image(part, from_north, from_south, valid)
    out[...] = image
    east[...], west[...] = edge_tiles(maskf * image)
    if step == 1:
        up, down, north, south = refs[:4]
        q_north, q_south = refs[-2:]
        mask_north, mask_south = north[HMAX:], south[HMAX:]
        q_north[...] = mask_north * (from_north[HMAX:] + mask_north * up[:HMAX])
        q_south[...] = mask_south * (from_south[HMAX:] + mask_south * down[:HMAX])


def sum_kernel(parts, out):
    out[...] = jnp.broadcast_to(jnp.sum(parts[...], axis=0, keepdims=True), out.shape)


def solve_kernel(parts, v0, v1, v2, part, from_north, from_south, valid, weights, residual):
    sums = jnp.sum(parts[...], axis=0)
    lane = lanes(sums.shape)
    gram = {}
    for k, (i, j) in enumerate(GRAM + [(2, 3)]):
        value = jnp.sum(jnp.where(lane == k, sums, 0.0), keepdims=True)
        gram[i, j] = gram[j, i] = value
    gram[0, 3], gram[1, 3] = gram[1, 2], gram[2, 2]

    def inner(a, b):
        total = None
        for i, x in a.items():
            for j, y in b.items():
                term = x * y * gram[i, j]
                total = term if total is None else total + term
        return total

    def combine(a, scale, b):
        out = dict(a)
        for i, y in b.items():
            out[i] = out[i] + scale * y if i in out else scale * y
        return out

    one = jnp.ones((1, 1), jnp.float32)
    w, r, d = {}, {0: one}, {0: one}
    now = inner(r, r)
    for step in range(3):
        image = {i + 1: x for i, x in d.items()}
        alpha = now / inner(d, image)
        w = combine(w, alpha, d)
        r = combine(r, -alpha, image)
        if step < 2:
            later = inner(r, r)
            d = combine(r, later / now, d)
            now = later
    basis = [v0[...], v1[...], v2[...], whole_image(part, from_north, from_south, valid)[0]]
    weights[...] = w[0] * basis[0] + w[1] * basis[1] + w[2] * basis[2]
    residual[...] = r[0] * basis[0] + r[1] * basis[1] + r[2] * basis[2] + r[3] * basis[3]


def call(kernel, outs, *args, name=None, flops=0, **more):
    return pl.pallas_call(
        kernel,
        out_shape=outs,
        compiler_params=pltpu.CompilerParams(vmem_limit_bytes=VMEM_LIMIT),
        cost_estimate=pl.CostEstimate(
            flops=flops, transcendentals=0, bytes_accessed=sum(a.size * a.dtype.itemsize for a in args)
        ),
        name=name or kernel.__name__,
        **more,
    )(*args)


def shards(ensemble, right_side, obs_error, valid, halfwidth):
    members, rows, cols = ensemble.shape
    quads, planes = members // 4, members // 2
    bf16 = functools.partial(jax.ShapeDtypeStruct, dtype=jnp.bfloat16)
    f32 = functools.partial(jax.ShapeDtypeStruct, dtype=jnp.float32)
    lon_band, side_band = lon_bands(halfwidth[0], cols)
    lat = lat_band(halfwidth[1], rows)
    q = valid.astype(jnp.float32) * right_side
    south, north = call(rows_kernel, [bf16((members, HMAX, cols))] * 2, ensemble)
    above = shift(south, "lat", 1, False)
    below = shift(north, "lat", -1, False)
    anywhere, plain = pl.BlockSpec(memory_space=pl.ANY), pl.BlockSpec(memory_space=pltpu.VMEM)
    east, west = call(
        columns_kernel, [bf16((quads + 3, rows, cols))] * 2, ensemble, q, south, north,
        in_specs=[plain, plain, anywhere, anywhere],
    )
    from_west = shift(east, LON, 1, True)
    from_east = shift(west, LON, -1, True)
    sides, q_sides = call(
        sides_kernel, [bf16((planes, rows, cols)), f32((rows, cols))], from_west, from_east
    )
    around = [q_sides]
    vectors, more = [right_side], []
    flops = 8 * members * rows * cols * (cols + rows)
    for step in range(3):
        vector = vectors[-1]
        message = f32((2 * HMAX if step < 2 else HMAX, cols))
        outs = [f32((rows, cols)), message, message]
        part, up, down = call(
            functools.partial(taper_kernel, step), outs,
            vector, valid, obs_error, *around, ensemble, sides, above, below, lon_band,
            side_band, lat, name=f"taper_{step}", flops=flops,
        )
        from_north = shift(down, "lat", 1, False)
        from_south = shift(up, "lat", -1, False)
        if step == 2:
            break
        outs = [f32((rows, cols))] * 3
        if step == 1:
            outs += [f32((HMAX, cols))] * 2
            more = [up, down] + masks
        image, east, west, *more = call(
            functools.partial(finish_kernel, step), outs, part, from_north, from_south, valid,
            *more, name=f"finish_{step}",
        )
        masks = [from_north, from_south]
        vectors.append(image)
        around = [shift(east, LON, 1, True), shift(west, LON, -1, True)]
    gram = call(
        gram_kernel, f32((lax.axis_size("far") * lax.axis_size("lat"), 1, 128)),
        *vectors, part, up, down, *more,
    )
    parts = lax.all_to_all(gram, ("far", "lat"), 0, 0)
    parts = call(sum_kernel, f32((lax.axis_size("near"), 1, 128)), parts)
    parts = lax.all_to_all(parts, "near", 0, 0)
    return tuple(
        call(
            solve_kernel, [f32((rows, cols))] * 2, parts, *vectors, part, from_north, from_south,
            valid,
        )
    )


def solution(mesh):
    devices = mesh.devices
    parts = 2 if devices.shape[0] % 2 == 0 else 1
    mesh = Mesh(
        devices.reshape(parts, devices.shape[0] // parts, devices.shape[1]), LON + ("lat",)
    )
    in_specs = (P(None, "lat", LON), P("lat", LON), P("lat", LON), P("lat", LON), P())
    out_specs = (P("lat", LON), P("lat", LON))
    return jax.shard_map(shards, mesh=mesh, in_specs=in_specs, out_specs=out_specs, check_vma=False)
```

```python
import functools

import jax
import jax.numpy as jnp
from jax import lax
from jax.experimental import pallas as pl
from jax.experimental.pallas import tpu as pltpu
from jax.sharding import Mesh
from jax.sharding import PartitionSpec as P

HMAX = 32
VMEM_LIMIT = 40 * 1024 * 1024


LON = ("far", "near")


def swap(cells, axis, second, closed):
    count = lax.axis_size(axis)
    partner = [((i - second) ^ 1) + second for i in range(count)]
    pairs = [(i, j % count) for i, j in enumerate(partner) if closed or 0 <= j < count]
    return lax.ppermute(cells, axis, pairs)


def taper_weight(offset, half):
    offset = offset.astype(jnp.float32)
    scale = half.astype(jnp.float32)
    ratio = offset / scale
    return jnp.where(jnp.abs(offset) <= scale, jnp.exp(-4.5 * ratio * ratio), 0.0).astype(
        jnp.bfloat16
    )


def lon_bands(half, cols, odd):
    lane = jnp.arange(cols)
    own = taper_weight(lane[:, None] - lane[None, :], half)
    first = lane % 64 < 32
    strip = jnp.where(first == (odd == 1), lane % 32 - HMAX, cols + lane % 32)
    both = jnp.arange(2 * cols)
    weight = taper_weight(strip[:, None] - both[None, :] % cols, half)
    keep = lane[:, None] // 64 == both[None, :] // cols
    side = jnp.where(keep, weight, jnp.zeros((), jnp.bfloat16))
    return jnp.concatenate([own, own]), jnp.concatenate([side, side])


def lat_band(half, rows, odd):
    row = jnp.arange(rows)
    halo = jnp.arange(HMAX)
    north, south = halo - HMAX, rows + halo
    target = jnp.concatenate(
        [row, jnp.where(odd == 1, north, south), jnp.where(odd == 1, south, north)]
    )
    source = jnp.concatenate([row, row])
    return taper_weight(source[None, :] - target[:, None], half)


def split3(x):
    hi = x.astype(jnp.bfloat16)
    rest = x - hi.astype(jnp.float32)
    mid = rest.astype(jnp.bfloat16)
    low = (rest - mid.astype(jnp.float32)).astype(jnp.bfloat16)
    return hi, mid, low


def join3(ref, first):
    parts = [ref[first + k].astype(jnp.float32) for k in range(3)]
    return parts[0] + parts[1] + parts[2]


def lanes(shape):
    return lax.broadcasted_iota(jnp.int32, shape, len(shape) - 1)


def edge_tiles(q, odd):
    lane = lanes(q.shape)
    right = jnp.where(lane >= 96, q, 0.0)
    right = right + pltpu.roll(right, 64, 1)
    right = right + pltpu.roll(right, 32, 1)
    left = jnp.where(lane < 32, q, 0.0)
    left = left + pltpu.roll(left, 64, 1)
    left = left + pltpu.roll(left, 32, 1)
    west_first = odd[0:1, :] == 1
    return jnp.where(west_first, left, right), jnp.where(west_first, right, left)


def edge_rows(x, odd):
    top, bottom = x[:HMAX], x[x.shape[0] - HMAX :]
    north_first = odd[8:9, :] == 1
    return jnp.where(north_first, top, bottom), jnp.where(north_first, bottom, top)


def rows_kernel(odd, ens, second, first):
    rows = ens.shape[1]
    north_first = odd[8:9, :] == 1
    for m in range(ens.shape[0]):
        top, bottom = ens[m, :HMAX, :], ens[m, rows - HMAX :, :]
        first[m] = jnp.where(north_first, top, bottom)
        second[m] = jnp.where(north_first, bottom, top)


def columns_kernel(odd, ens, q, _, __, second, first):
    members, rows, cols = ens.shape
    source = lax.broadcasted_iota(jnp.int32, (4 * cols, 2 * cols), 0)
    target = lax.broadcasted_iota(jnp.int32, (4 * cols, 2 * cols), 1)
    lane = target % cols
    flag = odd[0:1, :]
    east = 96 * jnp.concatenate([flag, flag], axis=1)
    wanted = (lane // 32) * cols + lane % 32 + jnp.where(target < cols, 96 - east, east)
    select = jnp.where(source == wanted, 1.0, 0.0).astype(jnp.bfloat16)
    quads = jnp.concatenate(
        [
            jnp.concatenate([ens[4 * i + g] for g in range(4)], axis=1)
            for i in range(members // 4)
        ],
        axis=0,
    )
    both = jnp.dot(quads, select, preferred_element_type=jnp.float32).astype(jnp.bfloat16)
    for i in range(members // 4):
        first[i] = both[rows * i : rows * (i + 1), :cols]
        second[i] = both[rows * i : rows * (i + 1), cols:]
    for ref, tile in zip((first, second), edge_tiles(q[...], odd)):
        for k, part in enumerate(split3(tile)):
            ref[members // 4 + k] = part


def sides_kernel(from_second, from_first, sides, q_sides):
    planes, rows, cols = sides.shape
    quads = planes // 2
    source = lax.broadcasted_iota(jnp.int32, (2 * cols, 2 * cols), 0)
    target = lax.broadcasted_iota(jnp.int32, (2 * cols, 2 * cols), 1)
    wanted = (target // 64) * 32 + target % 32 + jnp.where(target % 64 < 32, 0, cols)
    select = jnp.where(source == wanted, 1.0, 0.0).astype(jnp.bfloat16)
    pairs = jnp.concatenate(
        [jnp.concatenate([from_first[i], from_second[i]], axis=1) for i in range(quads)], axis=0
    )
    both = jnp.dot(pairs, select, preferred_element_type=jnp.float32).astype(jnp.bfloat16)
    for i in range(quads):
        for k in range(2):
            sides[2 * i + k] = both[rows * i : rows * (i + 1), k * cols : (k + 1) * cols]
    first = lanes((rows, cols)) % 64 < 32
    q_sides[...] = jnp.where(first, join3(from_first, quads), join3(from_second, quads))


def gram_lanes(vectors, last):
    lane = lanes((1, 128))
    out = jnp.where(lane == len(GRAM), last, 0.0)
    for k, (i, j) in enumerate(GRAM):
        out = jnp.where(lane == k, jnp.sum(vectors[i] * vectors[j], keepdims=True), out)
    return out


GRAM = [(0, 0), (0, 1), (0, 2), (1, 1), (1, 2), (2, 2)]


def high_low(x):
    high = x.astype(jnp.bfloat16)
    return high, (x - high.astype(jnp.float32)).astype(jnp.bfloat16)


def taper_kernel(step, odd, vector, valid, obs_error, *refs):
    if step == 0:
        q_sides, refs = refs[0][...], refs[1:]
    else:
        second, first, refs = refs[0], refs[1], refs[2:]
        q_sides = jnp.where(lanes(first.shape) % 64 < 32, first[...], second[...])
    ens, sides, rows_second, rows_first, lon_band, side_band, lat = refs[:7]
    part, to_second, to_first = refs[-3:]
    members, rows, cols = ens.shape
    count = members // 2
    maskf = valid[...].astype(jnp.float32)
    q = maskf * vector[...]
    side = jnp.concatenate(
        [
            jnp.concatenate(high_low(sides[j].astype(jnp.float32) * q_sides), axis=1)
            for j in range(count)
        ],
        axis=0,
    )
    side = jnp.dot(side, side_band[...], preferred_element_type=jnp.float32)
    main = jnp.concatenate(
        [
            jnp.concatenate(high_low(ens[m].astype(jnp.float32) * q), axis=1)
            for m in range(members)
        ],
        axis=0,
    )
    main = jnp.dot(main, lon_band[...], preferred_element_type=jnp.float32)
    total = jnp.zeros((rows + 2 * HMAX, cols), jnp.float32)
    for j in range(count):
        first = [
            main[rows * (2 * j + k) : rows * (2 * j + k + 1)]
            + side[rows * j : rows * (j + 1), cols * k : cols * (k + 1)]
            for k in range(2)
        ]
        pair = jnp.concatenate(high_low(jnp.concatenate(first, axis=1)), axis=0)
        second = jnp.dot(lat[...], pair, preferred_element_type=jnp.float32)
        for k in range(2):
            m = 2 * j + k
            there = jnp.concatenate([ens[m], rows_first[m], rows_second[m]], axis=0).astype(jnp.float32)
            total = total + there * second[:, cols * k : cols * (k + 1)]
    total = total / (members - 1)
    image = maskf * total[:rows] + obs_error[...] * vector[...]
    to_first[:HMAX] = total[rows : rows + HMAX]
    to_second[:HMAX] = total[rows + HMAX :]
    part[...] = image
    if step < 2:
        to_first[HMAX:], to_second[HMAX:] = edge_rows(maskf if step == 0 else image, odd)


def gram_kernel(v0, v1, v2, part, to_second, to_first, q_second, q_first, gram):
    vectors = [v0[...], v1[...], v2[...]]
    around = q_second[...] * to_second[...] + q_first[...] * to_first[...]
    last = jnp.sum(vectors[2] * part[...], keepdims=True) + jnp.sum(around, keepdims=True)
    gram[...] = jnp.broadcast_to(gram_lanes(vectors, last)[None], gram.shape)


def whole_image(odd, part, from_second, from_first, valid):
    first, second = from_first[:HMAX], from_second[:HMAX]
    north_first = odd[8:9, :] == 1
    around = jnp.concatenate(
        [jnp.where(north_first, first, second), jnp.where(north_first, second, first)], axis=0
    )
    maskf = valid[...].astype(jnp.float32)
    return part[...] + maskf * around, maskf


def finish_kernel(step, odd, part, from_second, from_first, valid, *refs):
    out, second, first = refs[-5:-2] if step == 1 else refs
    image, maskf = whole_image(odd, part, from_second, from_first, valid)
    out[...] = image
    first[...], second[...] = edge_tiles(maskf * image, odd)
    if step == 1:
        to_second, to_first, masks_second, masks_first = refs[:4]
        q_second, q_first = refs[-2:]
        mask = masks_second[HMAX:]
        q_second[...] = mask * (from_second[HMAX:] + mask * to_second[:HMAX])
        mask = masks_first[HMAX:]
        q_first[...] = mask * (from_first[HMAX:] + mask * to_first[:HMAX])


def sum_kernel(parts, out):
    out[...] = jnp.broadcast_to(jnp.sum(parts[...], axis=0, keepdims=True), out.shape)


def solve_kernel(odd, parts, v0, v1, v2, part, from_second, from_first, valid, weights, residual):
    sums = jnp.sum(parts[...], axis=0)
    lane = lanes(sums.shape)
    gram = {}
    for k, (i, j) in enumerate(GRAM + [(2, 3)]):
        value = jnp.sum(jnp.where(lane == k, sums, 0.0), keepdims=True)
        gram[i, j] = gram[j, i] = value
    gram[0, 3], gram[1, 3] = gram[1, 2], gram[2, 2]

    def inner(a, b):
        total = None
        for i, x in a.items():
            for j, y in b.items():
                term = x * y * gram[i, j]
                total = term if total is None else total + term
        return total

    def combine(a, scale, b):
        out = dict(a)
        for i, y in b.items():
            out[i] = out[i] + scale * y if i in out else scale * y
        return out

    one = jnp.ones((1, 1), jnp.float32)
    w, r, d = {}, {0: one}, {0: one}
    now = inner(r, r)
    for step in range(3):
        image = {i + 1: x for i, x in d.items()}
        alpha = now / inner(d, image)
        w = combine(w, alpha, d)
        r = combine(r, -alpha, image)
        if step < 2:
            later = inner(r, r)
            d = combine(r, later / now, d)
            now = later
    basis = [v0[...], v1[...], v2[...], whole_image(odd, part, from_second, from_first, valid)[0]]
    weights[...] = w[0] * basis[0] + w[1] * basis[1] + w[2] * basis[2]
    residual[...] = r[0] * basis[0] + r[1] * basis[1] + r[2] * basis[2] + r[3] * basis[3]


def call(kernel, outs, *args, name=None, flops=0, **more):
    return pl.pallas_call(
        kernel,
        out_shape=outs,
        compiler_params=pltpu.CompilerParams(vmem_limit_bytes=VMEM_LIMIT),
        cost_estimate=pl.CostEstimate(
            flops=flops, transcendentals=0, bytes_accessed=sum(a.size * a.dtype.itemsize for a in args)
        ),
        name=name or kernel.__name__,
        **more,
    )(*args)


def shards(ensemble, right_side, obs_error, valid, halfwidth):
    members, rows, cols = ensemble.shape
    quads, planes = members // 4, members // 2
    bf16 = functools.partial(jax.ShapeDtypeStruct, dtype=jnp.bfloat16)
    f32 = functools.partial(jax.ShapeDtypeStruct, dtype=jnp.float32)
    odd_lon, odd_lat = lax.axis_index(LON) % 2, lax.axis_index("lat") % 2
    odd = jnp.where(jnp.arange(16)[:, None] < 8, odd_lon, odd_lat)
    odd = jnp.broadcast_to(odd, (16, cols)).astype(jnp.int32)
    lon_band, side_band = lon_bands(halfwidth[0], cols, odd_lon)
    lat = lat_band(halfwidth[1], rows, odd_lat)
    plain = pl.BlockSpec(memory_space=pltpu.VMEM)
    anywhere = pl.BlockSpec(memory_space=pl.ANY)

    def with_odd(kernel, outs, *args, **more):
        return call(kernel, outs, odd, *args, in_specs=[plain] * (1 + len(args)), **more)

    q = valid.astype(jnp.float32) * right_side
    second, first = with_odd(rows_kernel, [bf16((members, HMAX, cols))] * 2, ensemble)
    rows_second = swap(second, "lat", 1, False)
    rows_first = swap(first, "lat", 0, False)
    second, first = call(
        columns_kernel, [bf16((quads + 3, rows, cols))] * 2, odd, ensemble, q, second, first,
        in_specs=[plain, plain, plain, anywhere, anywhere],
    )
    sides, q_sides = call(
        sides_kernel, [bf16((planes, rows, cols)), f32((rows, cols))],
        swap(second, LON, 1, True), swap(first, LON, 0, True),
    )
    around = [q_sides]
    vectors, more = [right_side], []
    flops = 8 * members * rows * cols * (cols + rows)
    for step in range(3):
        vector = vectors[-1]
        message = f32((2 * HMAX if step < 2 else HMAX, cols))
        part, to_second, to_first = with_odd(
            functools.partial(taper_kernel, step), [f32((rows, cols)), message, message],
            vector, valid, obs_error, *around, ensemble, sides, rows_second, rows_first,
            lon_band, side_band, lat, name=f"taper_{step}", flops=flops,
        )
        from_second = swap(to_second, "lat", 1, False)
        from_first = swap(to_first, "lat", 0, False)
        if step == 2:
            break
        outs = [f32((rows, cols))] * 3
        if step == 1:
            outs += [f32((HMAX, cols))] * 2
            more = [to_second, to_first] + masks
        image, second, first, *more = with_odd(
            functools.partial(finish_kernel, step), outs, part, from_second, from_first, valid,
            *more, name=f"finish_{step}",
        )
        masks = [from_second, from_first]
        vectors.append(image)
        around = [swap(second, LON, 1, True), swap(first, LON, 0, True)]
    gram = call(
        gram_kernel, f32((lax.axis_size("far") * lax.axis_size("lat"), 1, 128)),
        *vectors, part, to_second, to_first, *more,
    )
    parts = lax.all_to_all(gram, ("far", "lat"), 0, 0)
    parts = call(sum_kernel, f32((lax.axis_size("near"), 1, 128)), parts)
    parts = lax.all_to_all(parts, "near", 0, 0)
    return tuple(
        with_odd(
            solve_kernel, [f32((rows, cols))] * 2, parts, *vectors, part, from_second,
            from_first, valid,
        )
    )


def solution(mesh):
    devices = mesh.devices
    parts = 2 if devices.shape[0] % 2 == 0 else 1
    mesh = Mesh(
        devices.reshape(parts, devices.shape[0] // parts, devices.shape[1]), LON + ("lat",)
    )
    in_specs = (P(None, "lat", LON), P("lat", LON), P("lat", LON), P("lat", LON), P())
    out_specs = (P("lat", LON), P("lat", LON))
    return jax.shard_map(shards, mesh=mesh, in_specs=in_specs, out_specs=out_specs, check_vma=False)
```

```python
import functools

import jax
import jax.numpy as jnp
from jax import lax
from jax.experimental import pallas as pl
from jax.experimental.pallas import tpu as pltpu
from jax.sharding import Mesh
from jax.sharding import PartitionSpec as P

HMAX = 32
VMEM_LIMIT = 40 * 1024 * 1024


LON = ("far", "near")


def swap(cells, axis, second, closed):
    count = lax.axis_size(axis)
    partner = [((i - second) ^ 1) + second for i in range(count)]
    pairs = [(i, j % count) for i, j in enumerate(partner) if closed or 0 <= j < count]
    return lax.ppermute(cells, axis, pairs)


def taper_weight(offset, half):
    offset = offset.astype(jnp.float32)
    scale = half.astype(jnp.float32)
    ratio = offset / scale
    return jnp.where(jnp.abs(offset) <= scale, jnp.exp(-4.5 * ratio * ratio), 0.0).astype(
        jnp.bfloat16
    )


def lon_bands(half, cols, odd):
    lane = jnp.arange(cols)
    own = taper_weight(lane[:, None] - lane[None, :], half)
    first = lane % 64 < 32
    strip = jnp.where(first == (odd == 1), lane % 32 - HMAX, cols + lane % 32)
    both = jnp.arange(2 * cols)
    weight = taper_weight(strip[:, None] - both[None, :] % cols, half)
    keep = lane[:, None] // 64 == both[None, :] // cols
    side = jnp.where(keep, weight, jnp.zeros((), jnp.bfloat16))
    return jnp.concatenate([own, own]), jnp.concatenate([side, side])


def lat_band(half, rows, odd):
    row = jnp.arange(rows)
    halo = jnp.arange(HMAX)
    north, south = halo - HMAX, rows + halo
    target = jnp.concatenate(
        [jnp.where(odd == 1, north, south), jnp.where(odd == 1, south, north)]
    )
    own = jnp.where(odd == 1, row, (row + HMAX) % rows)
    target = jnp.concatenate([own, target])
    source = jnp.concatenate([own, own])
    return taper_weight(source[None, :] - target[:, None], half)


def joined(ref, first):
    return ref[first].astype(jnp.float32) + ref[first + 1].astype(jnp.float32)


def lanes(shape):
    return lax.broadcasted_iota(jnp.int32, shape, len(shape) - 1)


def edge_tiles(q, odd):
    lane = lanes(q.shape)
    right = jnp.where(lane >= 96, q, 0.0)
    right = right + pltpu.roll(right, 64, 1)
    right = right + pltpu.roll(right, 32, 1)
    left = jnp.where(lane < 32, q, 0.0)
    left = left + pltpu.roll(left, 64, 1)
    left = left + pltpu.roll(left, 32, 1)
    west_first = odd[0:1, :] == 1
    return jnp.where(west_first, left, right), jnp.where(west_first, right, left)


def by_partner(x, odd):
    turned = jnp.concatenate([x[HMAX:], x[:HMAX]], axis=0)
    return jnp.where(odd[1:2, :] == 1, x, turned)


def edge_rows(x, odd):
    top, bottom = x[:HMAX], x[x.shape[0] - HMAX :]
    north_first = odd[1:2, :] == 1
    return jnp.where(north_first, top, bottom), jnp.where(north_first, bottom, top)


def rows_kernel(odd, ens, second, first):
    rows = ens.shape[1]
    north_first = odd[1:2, :] == 1
    for m in range(ens.shape[0]):
        top, bottom = ens[m, :HMAX, :], ens[m, rows - HMAX :, :]
        first[m] = jnp.where(north_first, top, bottom)
        second[m] = jnp.where(north_first, bottom, top)


def columns_kernel(odd, q, half_second, half_first, second, first):
    members, half, cols = half_first.shape
    rows = 2 * half
    source = lax.broadcasted_iota(jnp.int32, (4 * cols, 2 * cols), 0)
    target = lax.broadcasted_iota(jnp.int32, (4 * cols, 2 * cols), 1)
    lane = target % cols
    flag = odd[0:1, :]
    east = 96 * jnp.concatenate([flag, flag], axis=1)
    wanted = (lane // 32) * cols + lane % 32 + jnp.where(target < cols, 96 - east, east)
    select = jnp.where(source == wanted, 1.0, 0.0).astype(jnp.bfloat16)
    quads = jnp.concatenate(
        [
            jnp.concatenate([ref[4 * i + g] for g in range(4)], axis=1)
            for i in range(members // 4)
            for ref in (half_first, half_second)
        ],
        axis=0,
    )
    both = jnp.dot(quads, select, preferred_element_type=jnp.float32).astype(jnp.bfloat16)
    for i in range(members // 4):
        first[i] = both[rows * i : rows * (i + 1), :cols]
        second[i] = both[rows * i : rows * (i + 1), cols:]
    for ref, tile in zip((first, second), edge_tiles(by_partner(q[...], odd), odd)):
        for k, part in enumerate(high_low(tile)):
            ref[members // 4 + k] = part


def sides_kernel(from_second, from_first, sides, q_sides):
    planes, rows, cols = sides.shape
    quads = planes // 2
    source = lax.broadcasted_iota(jnp.int32, (2 * cols, 2 * cols), 0)
    target = lax.broadcasted_iota(jnp.int32, (2 * cols, 2 * cols), 1)
    wanted = (target // 64) * 32 + target % 32 + jnp.where(target % 64 < 32, 0, cols)
    select = jnp.where(source == wanted, 1.0, 0.0).astype(jnp.bfloat16)
    pairs = jnp.concatenate(
        [jnp.concatenate([from_first[i], from_second[i]], axis=1) for i in range(quads)], axis=0
    )
    both = jnp.dot(pairs, select, preferred_element_type=jnp.float32).astype(jnp.bfloat16)
    for i in range(quads):
        for k in range(2):
            sides[2 * i + k] = both[rows * i : rows * (i + 1), k * cols : (k + 1) * cols]
    first = lanes((rows, cols)) % 64 < 32
    q_sides[...] = jnp.where(first, joined(from_first, quads), joined(from_second, quads))


def gram_lanes(vectors, last):
    lane = lanes((1, 128))
    out = jnp.where(lane == len(GRAM), last, 0.0)
    for k, (i, j) in enumerate(GRAM):
        out = jnp.where(lane == k, jnp.sum(vectors[i] * vectors[j], keepdims=True), out)
    return out


GRAM = [(0, 0), (0, 1), (0, 2), (1, 1), (1, 2), (2, 2)]


def high_low(x):
    high = x.astype(jnp.bfloat16)
    return high, (x - high.astype(jnp.float32)).astype(jnp.bfloat16)


def taper_kernel(step, odd, vector, valid, obs_error, *refs):
    if step == 0:
        q_sides, refs = refs[0][...], refs[1:]
    else:
        second, first, refs = refs[0], refs[1], refs[2:]
        q_sides = jnp.where(lanes(first.shape) % 64 < 32, first[...], second[...])
    half_second, half_first, sides, rows_second, rows_first = refs[:5]
    lon_band, side_band, lat = refs[5:8]
    part, to_second, to_first = refs[-3:]
    rows, cols = vector.shape
    members = half_first.shape[0]
    count = members // 2
    maskf = valid[...].astype(jnp.float32)
    q = by_partner(maskf * vector[...], odd)
    ens = [jnp.concatenate([half_first[m], half_second[m]], axis=0) for m in range(members)]
    side = jnp.concatenate(
        [
            jnp.concatenate(high_low(sides[j].astype(jnp.float32) * q_sides), axis=1)
            for j in range(count)
        ],
        axis=0,
    )
    side = jnp.dot(side, side_band[...], preferred_element_type=jnp.float32)
    main = jnp.concatenate(
        [
            jnp.concatenate(high_low(ens[m].astype(jnp.float32) * q), axis=1)
            for m in range(members)
        ],
        axis=0,
    )
    main = jnp.dot(main, lon_band[...], preferred_element_type=jnp.float32)
    total = jnp.zeros((rows + 2 * HMAX, cols), jnp.float32)
    for j in range(count):
        first = [
            main[rows * (2 * j + k) : rows * (2 * j + k + 1)]
            + side[rows * j : rows * (j + 1), cols * k : cols * (k + 1)]
            for k in range(2)
        ]
        pair = jnp.concatenate(high_low(jnp.concatenate(first, axis=1)), axis=0)
        second = jnp.dot(lat[...], pair, preferred_element_type=jnp.float32)
        for k in range(2):
            m = 2 * j + k
            there = jnp.concatenate([ens[m], rows_first[m], rows_second[m]], axis=0).astype(jnp.float32)
            total = total + there * second[:, cols * k : cols * (k + 1)]
    total = total / (members - 1)
    image = maskf * by_partner(total[:rows], odd) + obs_error[...] * vector[...]
    to_first[:HMAX] = total[rows : rows + HMAX]
    to_second[:HMAX] = total[rows + HMAX :]
    part[...] = image
    if step < 2:
        to_first[HMAX:], to_second[HMAX:] = edge_rows(maskf if step == 0 else image, odd)


def gram_kernel(v0, v1, v2, part, to_second, to_first, q_second, q_first, gram):
    vectors = [v0[...], v1[...], v2[...]]
    around = q_second[...] * to_second[...] + q_first[...] * to_first[...]
    last = jnp.sum(vectors[2] * part[...], keepdims=True) + jnp.sum(around, keepdims=True)
    gram[...] = jnp.broadcast_to(gram_lanes(vectors, last)[None], gram.shape)


def whole_image(odd, part, from_second, from_first, valid):
    first, second = from_first[:HMAX], from_second[:HMAX]
    north_first = odd[1:2, :] == 1
    around = jnp.concatenate(
        [jnp.where(north_first, first, second), jnp.where(north_first, second, first)], axis=0
    )
    maskf = valid[...].astype(jnp.float32)
    return part[...] + maskf * around, maskf


def finish_kernel(step, odd, part, from_second, from_first, valid, *refs):
    out, second, first = refs[-5:-2] if step == 1 else refs
    image, maskf = whole_image(odd, part, from_second, from_first, valid)
    out[...] = image
    first[...], second[...] = edge_tiles(by_partner(maskf * image, odd), odd)
    if step == 1:
        to_second, to_first, masks_second, masks_first = refs[:4]
        q_second, q_first = refs[-2:]
        mask = masks_second[HMAX:]
        q_second[...] = mask * (from_second[HMAX:] + mask * to_second[:HMAX])
        mask = masks_first[HMAX:]
        q_first[...] = mask * (from_first[HMAX:] + mask * to_first[:HMAX])


def sum_kernel(parts, out):
    out[...] = jnp.broadcast_to(jnp.sum(parts[...], axis=0, keepdims=True), out.shape)


def solve_kernel(odd, parts, v0, v1, v2, part, from_second, from_first, valid, weights, residual):
    sums = jnp.sum(parts[...], axis=0)
    lane = lanes(sums.shape)
    gram = {}
    for k, (i, j) in enumerate(GRAM + [(2, 3)]):
        value = jnp.sum(jnp.where(lane == k, sums, 0.0), keepdims=True)
        gram[i, j] = gram[j, i] = value
    gram[0, 3], gram[1, 3] = gram[1, 2], gram[2, 2]

    def inner(a, b):
        total = None
        for i, x in a.items():
            for j, y in b.items():
                term = x * y * gram[i, j]
                total = term if total is None else total + term
        return total

    def combine(a, scale, b):
        out = dict(a)
        for i, y in b.items():
            out[i] = out[i] + scale * y if i in out else scale * y
        return out

    one = jnp.ones((1, 1), jnp.float32)
    w, r, d = {}, {0: one}, {0: one}
    now = inner(r, r)
    for step in range(3):
        image = {i + 1: x for i, x in d.items()}
        alpha = now / inner(d, image)
        w = combine(w, alpha, d)
        r = combine(r, -alpha, image)
        if step < 2:
            later = inner(r, r)
            d = combine(r, later / now, d)
            now = later
    basis = [v0[...], v1[...], v2[...], whole_image(odd, part, from_second, from_first, valid)[0]]
    weights[...] = w[0] * basis[0] + w[1] * basis[1] + w[2] * basis[2]
    residual[...] = r[0] * basis[0] + r[1] * basis[1] + r[2] * basis[2] + r[3] * basis[3]


def call(kernel, outs, *args, name=None, flops=0, **more):
    return pl.pallas_call(
        kernel,
        out_shape=outs,
        compiler_params=pltpu.CompilerParams(vmem_limit_bytes=VMEM_LIMIT),
        cost_estimate=pl.CostEstimate(
            flops=flops, transcendentals=0, bytes_accessed=sum(a.size * a.dtype.itemsize for a in args)
        ),
        name=name or kernel.__name__,
        **more,
    )(*args)


def shards(ensemble, right_side, obs_error, valid, halfwidth):
    members, rows, cols = ensemble.shape
    quads, planes = members // 4, members // 2
    bf16 = functools.partial(jax.ShapeDtypeStruct, dtype=jnp.bfloat16)
    f32 = functools.partial(jax.ShapeDtypeStruct, dtype=jnp.float32)
    odd_lon, odd_lat = lax.axis_index(LON) % 2, lax.axis_index("lat") % 2
    odd = jnp.where(jnp.arange(8)[:, None] == 0, odd_lon, odd_lat)
    odd = jnp.broadcast_to(odd, (8, cols)).astype(jnp.int32)
    lon_band, side_band = lon_bands(halfwidth[0], cols, odd_lon)
    lat = lat_band(halfwidth[1], rows, odd_lat)
    plain = pl.BlockSpec(memory_space=pltpu.VMEM)

    def with_odd(kernel, outs, *args, **more):
        return call(kernel, outs, odd, *args, in_specs=[plain] * (1 + len(args)), **more)

    q = valid.astype(jnp.float32) * right_side
    halves = with_odd(rows_kernel, [bf16((members, HMAX, cols))] * 2, ensemble)
    rows_second = swap(halves[0], "lat", 1, False)
    rows_first = swap(halves[1], "lat", 0, False)
    second, first = with_odd(
        columns_kernel, [bf16((quads + 2, rows, cols))] * 2, q, *halves
    )
    sides, q_sides = call(
        sides_kernel, [bf16((planes, rows, cols)), f32((rows, cols))],
        swap(second, LON, 1, True), swap(first, LON, 0, True),
    )
    around = [q_sides]
    vectors, more = [right_side], []
    flops = 8 * members * rows * cols * (cols + rows)
    for step in range(3):
        vector = vectors[-1]
        message = f32((2 * HMAX if step < 2 else HMAX, cols))
        part, to_second, to_first = with_odd(
            functools.partial(taper_kernel, step), [f32((rows, cols)), message, message],
            vector, valid, obs_error, *around, *halves, sides, rows_second, rows_first,
            lon_band, side_band, lat, name=f"taper_{step}", flops=flops,
        )
        from_second = swap(to_second, "lat", 1, False)
        from_first = swap(to_first, "lat", 0, False)
        if step == 2:
            break
        outs = [f32((rows, cols))] * 3
        if step == 1:
            outs += [f32((HMAX, cols))] * 2
            more = [to_second, to_first] + masks
        image, second, first, *more = with_odd(
            functools.partial(finish_kernel, step), outs, part, from_second, from_first, valid,
            *more, name=f"finish_{step}",
        )
        masks = [from_second, from_first]
        vectors.append(image)
        around = [swap(second, LON, 1, True), swap(first, LON, 0, True)]
    gram = call(
        gram_kernel, f32((lax.axis_size("far") * lax.axis_size("lat"), 1, 128)),
        *vectors, part, to_second, to_first, *more,
    )
    parts = lax.all_to_all(gram, ("far", "lat"), 0, 0)
    parts = call(sum_kernel, f32((lax.axis_size("near"), 1, 128)), parts)
    parts = lax.all_to_all(parts, "near", 0, 0)
    return tuple(
        with_odd(
            solve_kernel, [f32((rows, cols))] * 2, parts, *vectors, part, from_second,
            from_first, valid,
        )
    )


def solution(mesh):
    devices = mesh.devices
    parts = 2 if devices.shape[0] % 2 == 0 else 1
    mesh = Mesh(
        devices.reshape(parts, devices.shape[0] // parts, devices.shape[1]), LON + ("lat",)
    )
    in_specs = (P(None, "lat", LON), P("lat", LON), P("lat", LON), P("lat", LON), P())
    out_specs = (P("lat", LON), P("lat", LON))
    return jax.shard_map(shards, mesh=mesh, in_specs=in_specs, out_specs=out_specs, check_vma=False)
```

```python
import functools

import jax
import jax.numpy as jnp
from jax import lax
from jax.experimental import pallas as pl
from jax.experimental.pallas import tpu as pltpu
from jax.sharding import Mesh
from jax.sharding import PartitionSpec as P

HMAX = 32
VMEM_LIMIT = 40 * 1024 * 1024


LON = ("far", "near")


def swap(cells, axis, second, closed):
    count = lax.axis_size(axis)
    partner = [((i - second) ^ 1) + second for i in range(count)]
    pairs = [(i, j % count) for i, j in enumerate(partner) if closed or 0 <= j < count]
    return lax.ppermute(cells, axis, pairs)


def taper_weight(offset, half):
    offset = offset.astype(jnp.float32)
    scale = half.astype(jnp.float32)
    ratio = offset / scale
    return jnp.where(jnp.abs(offset) <= scale, jnp.exp(-4.5 * ratio * ratio), 0.0).astype(
        jnp.bfloat16
    )


def lon_bands(half, cols, odd):
    lane = jnp.arange(cols)
    own = taper_weight(lane[:, None] - lane[None, :], half)
    first = lane % 64 < 32
    strip = jnp.where(first == (odd == 1), lane % 32 - HMAX, cols + lane % 32)
    both = jnp.arange(2 * cols)
    weight = taper_weight(strip[:, None] - both[None, :] % cols, half)
    keep = lane[:, None] // 64 == both[None, :] // cols
    side = jnp.where(keep, weight, jnp.zeros((), jnp.bfloat16))
    return jnp.concatenate([own, own]), jnp.concatenate([side, side])


def lat_band(half, rows, odd):
    row = jnp.arange(rows)
    halo = jnp.arange(HMAX)
    north, south = halo - HMAX, rows + halo
    target = jnp.concatenate(
        [jnp.where(odd == 1, north, south), jnp.where(odd == 1, south, north)]
    )
    own = jnp.where(odd == 1, row, (row + HMAX) % rows)
    target = jnp.concatenate([own, target])
    source = jnp.concatenate([own, own])
    return taper_weight(source[None, :] - target[:, None], half)


def joined(ref, first):
    return ref[first].astype(jnp.float32) + ref[first + 1].astype(jnp.float32)


def lanes(shape):
    return lax.broadcasted_iota(jnp.int32, shape, len(shape) - 1)


def edge_tiles(q, odd):
    lane = lanes(q.shape)
    right = jnp.where(lane >= 96, q, 0.0)
    right = right + pltpu.roll(right, 64, 1)
    right = right + pltpu.roll(right, 32, 1)
    left = jnp.where(lane < 32, q, 0.0)
    left = left + pltpu.roll(left, 64, 1)
    left = left + pltpu.roll(left, 32, 1)
    west_first = odd[0:1, :] == 1
    return jnp.where(west_first, left, right), jnp.where(west_first, right, left)


def by_partner(x, odd):
    turned = jnp.concatenate([x[HMAX:], x[:HMAX]], axis=0)
    return jnp.where(odd[1:2, :] == 1, x, turned)


def edge_rows(x, odd):
    top, bottom = x[:HMAX], x[x.shape[0] - HMAX :]
    north_first = odd[1:2, :] == 1
    return jnp.where(north_first, top, bottom), jnp.where(north_first, bottom, top)


def rows_kernel(odd, ens, second, first):
    rows = ens.shape[1]
    north_first = odd[1:2, :] == 1
    for m in range(ens.shape[0]):
        top, bottom = ens[m, :HMAX, :], ens[m, rows - HMAX :, :]
        first[m] = jnp.where(north_first, top, bottom)
        second[m] = jnp.where(north_first, bottom, top)


def after_kernel(*refs):
    del refs


def columns_kernel(odd, q, half_second, half_first, second, first):
    members, half, cols = half_first.shape
    rows = 2 * half
    source = lax.broadcasted_iota(jnp.int32, (4 * cols, 2 * cols), 0)
    target = lax.broadcasted_iota(jnp.int32, (4 * cols, 2 * cols), 1)
    lane = target % cols
    flag = odd[0:1, :]
    east = 96 * jnp.concatenate([flag, flag], axis=1)
    wanted = (lane // 32) * cols + lane % 32 + jnp.where(target < cols, 96 - east, east)
    select = jnp.where(source == wanted, 1.0, 0.0).astype(jnp.bfloat16)
    quads = jnp.concatenate(
        [
            jnp.concatenate([ref[4 * i + g] for g in range(4)], axis=1)
            for i in range(members // 4)
            for ref in (half_first, half_second)
        ],
        axis=0,
    )
    both = jnp.dot(quads, select, preferred_element_type=jnp.float32).astype(jnp.bfloat16)
    for i in range(members // 4):
        first[i] = both[rows * i : rows * (i + 1), :cols]
        second[i] = both[rows * i : rows * (i + 1), cols:]
    for ref, tile in zip((first, second), edge_tiles(by_partner(q[...], odd), odd)):
        for k, part in enumerate(high_low(tile)):
            ref[members // 4 + k] = part


def sides_kernel(from_second, from_first, sides, q_sides):
    planes, rows, cols = sides.shape
    quads = planes // 2
    source = lax.broadcasted_iota(jnp.int32, (2 * cols, 2 * cols), 0)
    target = lax.broadcasted_iota(jnp.int32, (2 * cols, 2 * cols), 1)
    wanted = (target // 64) * 32 + target % 32 + jnp.where(target % 64 < 32, 0, cols)
    select = jnp.where(source == wanted, 1.0, 0.0).astype(jnp.bfloat16)
    pairs = jnp.concatenate(
        [jnp.concatenate([from_first[i], from_second[i]], axis=1) for i in range(quads)], axis=0
    )
    both = jnp.dot(pairs, select, preferred_element_type=jnp.float32).astype(jnp.bfloat16)
    for i in range(quads):
        for k in range(2):
            sides[2 * i + k] = both[rows * i : rows * (i + 1), k * cols : (k + 1) * cols]
    first = lanes((rows, cols)) % 64 < 32
    q_sides[...] = jnp.where(first, joined(from_first, quads), joined(from_second, quads))


def gram_lanes(vectors, last):
    lane = lanes((1, 128))
    out = jnp.where(lane == len(GRAM), last, 0.0)
    for k, (i, j) in enumerate(GRAM):
        out = jnp.where(lane == k, jnp.sum(vectors[i] * vectors[j], keepdims=True), out)
    return out


GRAM = [(0, 0), (0, 1), (0, 2), (1, 1), (1, 2), (2, 2)]


def high_low(x):
    high = x.astype(jnp.bfloat16)
    return high, (x - high.astype(jnp.float32)).astype(jnp.bfloat16)


def taper_kernel(step, odd, vector, valid, obs_error, *refs):
    if step == 0:
        q_sides, refs = refs[0][...], refs[1:]
    else:
        second, first, refs = refs[0], refs[1], refs[2:]
        q_sides = jnp.where(lanes(first.shape) % 64 < 32, first[...], second[...])
    half_second, half_first, sides, rows_second, rows_first = refs[:5]
    lon_band, side_band, lat = refs[5:8]
    part, to_second, to_first = refs[-3:]
    rows, cols = vector.shape
    members = half_first.shape[0]
    count = members // 2
    maskf = valid[...].astype(jnp.float32)
    q = by_partner(maskf * vector[...], odd)
    ens = [jnp.concatenate([half_first[m], half_second[m]], axis=0) for m in range(members)]
    side = jnp.concatenate(
        [
            jnp.concatenate(high_low(sides[j].astype(jnp.float32) * q_sides), axis=1)
            for j in range(count)
        ],
        axis=0,
    )
    side = jnp.dot(side, side_band[...], preferred_element_type=jnp.float32)
    main = jnp.concatenate(
        [
            jnp.concatenate(high_low(ens[m].astype(jnp.float32) * q), axis=1)
            for m in range(members)
        ],
        axis=0,
    )
    main = jnp.dot(main, lon_band[...], preferred_element_type=jnp.float32)
    total = jnp.zeros((rows + 2 * HMAX, cols), jnp.float32)
    for j in range(count):
        first = [
            main[rows * (2 * j + k) : rows * (2 * j + k + 1)]
            + side[rows * j : rows * (j + 1), cols * k : cols * (k + 1)]
            for k in range(2)
        ]
        pair = jnp.concatenate(high_low(jnp.concatenate(first, axis=1)), axis=0)
        second = jnp.dot(lat[...], pair, preferred_element_type=jnp.float32)
        for k in range(2):
            m = 2 * j + k
            there = jnp.concatenate([ens[m], rows_first[m], rows_second[m]], axis=0).astype(jnp.float32)
            total = total + there * second[:, cols * k : cols * (k + 1)]
    total = total / (members - 1)
    image = maskf * by_partner(total[:rows], odd) + obs_error[...] * vector[...]
    to_first[:HMAX] = total[rows : rows + HMAX]
    to_second[:HMAX] = total[rows + HMAX :]
    part[...] = image
    if step < 2:
        to_first[HMAX:], to_second[HMAX:] = edge_rows(maskf if step == 0 else image, odd)


def gram_kernel(v0, v1, v2, part, to_second, to_first, q_second, q_first, gram):
    vectors = [v0[...], v1[...], v2[...]]
    around = q_second[...] * to_second[...] + q_first[...] * to_first[...]
    last = jnp.sum(vectors[2] * part[...], keepdims=True) + jnp.sum(around, keepdims=True)
    gram[...] = jnp.broadcast_to(gram_lanes(vectors, last)[None], gram.shape)


def whole_image(odd, part, from_second, from_first, valid):
    first, second = from_first[:HMAX], from_second[:HMAX]
    north_first = odd[1:2, :] == 1
    around = jnp.concatenate(
        [jnp.where(north_first, first, second), jnp.where(north_first, second, first)], axis=0
    )
    maskf = valid[...].astype(jnp.float32)
    return part[...] + maskf * around, maskf


def finish_kernel(step, odd, part, from_second, from_first, valid, *refs):
    out, second, first = refs[-5:-2] if step == 1 else refs
    image, maskf = whole_image(odd, part, from_second, from_first, valid)
    out[...] = image
    first[...], second[...] = edge_tiles(by_partner(maskf * image, odd), odd)
    if step == 1:
        to_second, to_first, masks_second, masks_first = refs[:4]
        q_second, q_first = refs[-2:]
        mask = masks_second[HMAX:]
        q_second[...] = mask * (from_second[HMAX:] + mask * to_second[:HMAX])
        mask = masks_first[HMAX:]
        q_first[...] = mask * (from_first[HMAX:] + mask * to_first[:HMAX])


def sum_kernel(parts, out):
    out[...] = jnp.broadcast_to(jnp.sum(parts[...], axis=0, keepdims=True), out.shape)


def solve_kernel(odd, parts, v0, v1, v2, part, from_second, from_first, valid, weights, residual):
    sums = jnp.sum(parts[...], axis=0)
    lane = lanes(sums.shape)
    gram = {}
    for k, (i, j) in enumerate(GRAM + [(2, 3)]):
        value = jnp.sum(jnp.where(lane == k, sums, 0.0), keepdims=True)
        gram[i, j] = gram[j, i] = value
    gram[0, 3], gram[1, 3] = gram[1, 2], gram[2, 2]

    def inner(a, b):
        total = None
        for i, x in a.items():
            for j, y in b.items():
                term = x * y * gram[i, j]
                total = term if total is None else total + term
        return total

    def combine(a, scale, b):
        out = dict(a)
        for i, y in b.items():
            out[i] = out[i] + scale * y if i in out else scale * y
        return out

    one = jnp.ones((1, 1), jnp.float32)
    w, r, d = {}, {0: one}, {0: one}
    now = inner(r, r)
    for step in range(3):
        image = {i + 1: x for i, x in d.items()}
        alpha = now / inner(d, image)
        w = combine(w, alpha, d)
        r = combine(r, -alpha, image)
        if step < 2:
            later = inner(r, r)
            d = combine(r, later / now, d)
            now = later
    basis = [v0[...], v1[...], v2[...], whole_image(odd, part, from_second, from_first, valid)[0]]
    weights[...] = w[0] * basis[0] + w[1] * basis[1] + w[2] * basis[2]
    residual[...] = r[0] * basis[0] + r[1] * basis[1] + r[2] * basis[2] + r[3] * basis[3]


def call(kernel, outs, *args, name=None, flops=0, **more):
    return pl.pallas_call(
        kernel,
        out_shape=outs,
        compiler_params=pltpu.CompilerParams(vmem_limit_bytes=VMEM_LIMIT),
        cost_estimate=pl.CostEstimate(
            flops=flops, transcendentals=0, bytes_accessed=sum(a.size * a.dtype.itemsize for a in args)
        ),
        name=name or kernel.__name__,
        **more,
    )(*args)


def shards(ensemble, right_side, obs_error, valid, halfwidth):
    members, rows, cols = ensemble.shape
    quads, planes = members // 4, members // 2
    bf16 = functools.partial(jax.ShapeDtypeStruct, dtype=jnp.bfloat16)
    f32 = functools.partial(jax.ShapeDtypeStruct, dtype=jnp.float32)
    odd_lon, odd_lat = lax.axis_index(LON) % 2, lax.axis_index("lat") % 2
    odd = jnp.where(jnp.arange(8)[:, None] == 0, odd_lon, odd_lat)
    odd = jnp.broadcast_to(odd, (8, cols)).astype(jnp.int32)
    lon_band, side_band = lon_bands(halfwidth[0], cols, odd_lon)
    lat = lat_band(halfwidth[1], rows, odd_lat)
    plain = pl.BlockSpec(memory_space=pltpu.VMEM)

    def with_odd(kernel, outs, *args, **more):
        return call(kernel, outs, odd, *args, in_specs=[plain] * (1 + len(args)), **more)

    q = valid.astype(jnp.float32) * right_side
    halves = with_odd(rows_kernel, [bf16((members, HMAX, cols))] * 2, ensemble)
    rows_second = swap(halves[0], "lat", 1, False)
    second, first = with_odd(
        columns_kernel, [bf16((quads + 2, rows, cols))] * 2, q, *halves
    )
    anywhere = pl.BlockSpec(memory_space=pl.ANY)
    half_first = pl.pallas_call(
        after_kernel, out_shape=bf16(halves[1].shape), in_specs=[anywhere] * 2,
        out_specs=anywhere, input_output_aliases={0: 0}, name="after_kernel",
    )(halves[1], first)
    halves = [halves[0], half_first]
    rows_first = swap(half_first, "lat", 0, False)
    sides, q_sides = call(
        sides_kernel, [bf16((planes, rows, cols)), f32((rows, cols))],
        swap(second, LON, 1, True), swap(first, LON, 0, True),
    )
    around = [q_sides]
    vectors, more = [right_side], []
    flops = 8 * members * rows * cols * (cols + rows)
    for step in range(3):
        vector = vectors[-1]
        message = f32((2 * HMAX if step < 2 else HMAX, cols))
        part, to_second, to_first = with_odd(
            functools.partial(taper_kernel, step), [f32((rows, cols)), message, message],
            vector, valid, obs_error, *around, *halves, sides, rows_second, rows_first,
            lon_band, side_band, lat, name=f"taper_{step}", flops=flops,
        )
        from_second = swap(to_second, "lat", 1, False)
        from_first = swap(to_first, "lat", 0, False)
        if step == 2:
            break
        outs = [f32((rows, cols))] * 3
        if step == 1:
            outs += [f32((HMAX, cols))] * 2
            more = [to_second, to_first] + masks
        image, second, first, *more = with_odd(
            functools.partial(finish_kernel, step), outs, part, from_second, from_first, valid,
            *more, name=f"finish_{step}",
        )
        masks = [from_second, from_first]
        vectors.append(image)
        around = [swap(second, LON, 1, True), swap(first, LON, 0, True)]
    gram = call(
        gram_kernel, f32((lax.axis_size("far") * lax.axis_size("lat"), 1, 128)),
        *vectors, part, to_second, to_first, *more,
    )
    parts = lax.all_to_all(gram, ("far", "lat"), 0, 0)
    parts = call(sum_kernel, f32((lax.axis_size("near"), 1, 128)), parts)
    parts = lax.all_to_all(parts, "near", 0, 0)
    return tuple(
        with_odd(
            solve_kernel, [f32((rows, cols))] * 2, parts, *vectors, part, from_second,
            from_first, valid,
        )
    )


def solution(mesh):
    devices = mesh.devices
    parts = 2 if devices.shape[0] % 2 == 0 else 1
    mesh = Mesh(
        devices.reshape(parts, devices.shape[0] // parts, devices.shape[1]), LON + ("lat",)
    )
    in_specs = (P(None, "lat", LON), P("lat", LON), P("lat", LON), P("lat", LON), P())
    out_specs = (P("lat", LON), P("lat", LON))
    return jax.shard_map(shards, mesh=mesh, in_specs=in_specs, out_specs=out_specs, check_vma=False)
```

```python
import functools

import jax
import jax.numpy as jnp
from jax import lax
from jax.experimental import pallas as pl
from jax.experimental.pallas import tpu as pltpu
from jax.sharding import Mesh
from jax.sharding import PartitionSpec as P

HMAX = 32
VMEM_LIMIT = 40 * 1024 * 1024


LON = ("far", "near")


def swap(cells, axis, second, closed):
    count = lax.axis_size(axis)
    partner = [((i - second) ^ 1) + second for i in range(count)]
    pairs = [(i, j % count) for i, j in enumerate(partner) if closed or 0 <= j < count]
    return lax.ppermute(cells, axis, pairs)


def taper_weight(offset, half):
    offset = offset.astype(jnp.float32)
    scale = half.astype(jnp.float32)
    ratio = offset / scale
    return jnp.where(jnp.abs(offset) <= scale, jnp.exp(-4.5 * ratio * ratio), 0.0).astype(
        jnp.bfloat16
    )


def lon_bands(half, cols, odd):
    lane = jnp.arange(cols)
    own = taper_weight(lane[:, None] - lane[None, :], half)
    first = lane % 64 < 32
    strip = jnp.where(first == (odd == 1), lane % 32 - HMAX, cols + lane % 32)
    both = jnp.arange(2 * cols)
    weight = taper_weight(strip[:, None] - both[None, :] % cols, half)
    keep = lane[:, None] // 64 == both[None, :] // cols
    side = jnp.where(keep, weight, jnp.zeros((), jnp.bfloat16))
    return jnp.concatenate([own, own]), jnp.concatenate([side, side])


def lat_band(half, rows, odd):
    row = jnp.arange(rows)
    halo = jnp.arange(HMAX)
    north, south = halo - HMAX, rows + halo
    target = jnp.concatenate(
        [jnp.where(odd == 1, north, south), jnp.where(odd == 1, south, north)]
    )
    own = jnp.where(odd == 1, row, (row + HMAX) % rows)
    target = jnp.concatenate([own, target])
    source = jnp.concatenate([own, own])
    return taper_weight(source[None, :] - target[:, None], half)


def joined(ref, first):
    return ref[first].astype(jnp.float32) + ref[first + 1].astype(jnp.float32)


def lanes(shape):
    return lax.broadcasted_iota(jnp.int32, shape, len(shape) - 1)


def edge_tiles(q, odd):
    lane = lanes(q.shape)
    right = jnp.where(lane >= 96, q, 0.0)
    right = right + pltpu.roll(right, 64, 1)
    right = right + pltpu.roll(right, 32, 1)
    left = jnp.where(lane < 32, q, 0.0)
    left = left + pltpu.roll(left, 64, 1)
    left = left + pltpu.roll(left, 32, 1)
    west_first = odd[0:1, :] == 1
    return jnp.where(west_first, left, right), jnp.where(west_first, right, left)


def by_partner(x, odd):
    turned = jnp.concatenate([x[HMAX:], x[:HMAX]], axis=0)
    return jnp.where(odd[1:2, :] == 1, x, turned)


def edge_rows(x, odd):
    top, bottom = x[:HMAX], x[x.shape[0] - HMAX :]
    north_first = odd[1:2, :] == 1
    return jnp.where(north_first, top, bottom), jnp.where(north_first, bottom, top)


def rows_kernel(odd, ens, second, first):
    rows = ens.shape[1]
    north_first = odd[1:2, :] == 1
    for m in range(ens.shape[0]):
        top, bottom = ens[m, :HMAX, :], ens[m, rows - HMAX :, :]
        first[m] = jnp.where(north_first, top, bottom)
        second[m] = jnp.where(north_first, bottom, top)


def columns_kernel(odd, q, half_second, half_first, second, first):
    members, half, cols = half_first.shape
    rows = 2 * half
    source = lax.broadcasted_iota(jnp.int32, (4 * cols, 2 * cols), 0)
    target = lax.broadcasted_iota(jnp.int32, (4 * cols, 2 * cols), 1)
    lane = target % cols
    flag = odd[0:1, :]
    east = 96 * jnp.concatenate([flag, flag], axis=1)
    wanted = (lane // 32) * cols + lane % 32 + jnp.where(target < cols, 96 - east, east)
    select = jnp.where(source == wanted, 1.0, 0.0).astype(jnp.bfloat16)
    quads = jnp.concatenate(
        [
            jnp.concatenate([ref[4 * i + g] for g in range(4)], axis=1)
            for i in range(members // 4)
            for ref in (half_first, half_second)
        ],
        axis=0,
    )
    both = jnp.dot(quads, select, preferred_element_type=jnp.float32).astype(jnp.bfloat16)
    for i in range(members // 4):
        first[i] = both[rows * i : rows * (i + 1), :cols]
        second[i] = both[rows * i : rows * (i + 1), cols:]
    for ref, tile in zip((first, second), edge_tiles(by_partner(q[...], odd), odd)):
        for k, part in enumerate(high_low(tile)):
            ref[members // 4 + k] = part


def sides_kernel(from_second, from_first, sides, q_sides):
    planes, rows, cols = sides.shape
    quads = planes // 2
    source = lax.broadcasted_iota(jnp.int32, (2 * cols, 2 * cols), 0)
    target = lax.broadcasted_iota(jnp.int32, (2 * cols, 2 * cols), 1)
    wanted = (target // 64) * 32 + target % 32 + jnp.where(target % 64 < 32, 0, cols)
    select = jnp.where(source == wanted, 1.0, 0.0).astype(jnp.bfloat16)
    pairs = jnp.concatenate(
        [jnp.concatenate([from_first[i], from_second[i]], axis=1) for i in range(quads)], axis=0
    )
    both = jnp.dot(pairs, select, preferred_element_type=jnp.float32).astype(jnp.bfloat16)
    for i in range(quads):
        for k in range(2):
            sides[2 * i + k] = both[rows * i : rows * (i + 1), k * cols : (k + 1) * cols]
    first = lanes((rows, cols)) % 64 < 32
    q_sides[...] = jnp.where(first, joined(from_first, quads), joined(from_second, quads))


def gram_lanes(vectors, last):
    lane = lanes((1, 128))
    out = jnp.where(lane == len(GRAM), last, 0.0)
    for k, (i, j) in enumerate(GRAM):
        out = jnp.where(lane == k, jnp.sum(vectors[i] * vectors[j], keepdims=True), out)
    return out


GRAM = [(0, 0), (0, 1), (0, 2), (1, 1), (1, 2), (2, 2)]


def high_low(x):
    high = x.astype(jnp.bfloat16)
    return high, (x - high.astype(jnp.float32)).astype(jnp.bfloat16)


def taper_kernel(step, odd, vector, valid, obs_error, *refs):
    if step == 0:
        q_sides, refs = refs[0][...], refs[1:]
    else:
        second, first, refs = refs[0], refs[1], refs[2:]
        q_sides = jnp.where(lanes(first.shape) % 64 < 32, first[...], second[...])
    half_second, half_first, sides, rows_second, rows_first = refs[:5]
    lon_band, side_band, lat = refs[5:8]
    part, to_second, to_first = refs[-3:]
    rows, cols = vector.shape
    members = half_first.shape[0]
    count = members // 2
    maskf = valid[...].astype(jnp.float32)
    q = by_partner(maskf * vector[...], odd)
    ens = [jnp.concatenate([half_first[m], half_second[m]], axis=0) for m in range(members)]
    side = jnp.concatenate(
        [
            jnp.concatenate(high_low(sides[j].astype(jnp.float32) * q_sides), axis=1)
            for j in range(count)
        ],
        axis=0,
    )
    side = jnp.dot(side, side_band[...], preferred_element_type=jnp.float32)
    main = jnp.concatenate(
        [
            jnp.concatenate(high_low(ens[m].astype(jnp.float32) * q), axis=1)
            for m in range(members)
        ],
        axis=0,
    )
    main = jnp.dot(main, lon_band[...], preferred_element_type=jnp.float32)
    total = jnp.zeros((rows + 2 * HMAX, cols), jnp.float32)
    for j in range(count):
        first = [
            main[rows * (2 * j + k) : rows * (2 * j + k + 1)]
            + side[rows * j : rows * (j + 1), cols * k : cols * (k + 1)]
            for k in range(2)
        ]
        pair = jnp.concatenate(high_low(jnp.concatenate(first, axis=1)), axis=0)
        second = jnp.dot(lat[...], pair, preferred_element_type=jnp.float32)
        terms = []
        for k in range(2):
            m = 2 * j + k
            there = jnp.concatenate([ens[m], rows_first[m], rows_second[m]], axis=0).astype(jnp.float32)
            terms.append(there * second[:, cols * k : cols * (k + 1)])
        total = total + (terms[0] + terms[1])
    total = total / (members - 1)
    image = maskf * by_partner(total[:rows], odd) + obs_error[...] * vector[...]
    to_first[:HMAX] = total[rows : rows + HMAX]
    to_second[:HMAX] = total[rows + HMAX :]
    part[...] = image
    if step < 2:
        to_first[HMAX:], to_second[HMAX:] = edge_rows(maskf if step == 0 else image, odd)


def gram_kernel(v0, v1, v2, part, to_second, to_first, q_second, q_first, gram):
    vectors = [v0[...], v1[...], v2[...]]
    around = q_second[...] * to_second[...] + q_first[...] * to_first[...]
    last = jnp.sum(vectors[2] * part[...], keepdims=True) + jnp.sum(around, keepdims=True)
    gram[...] = jnp.broadcast_to(gram_lanes(vectors, last)[None], gram.shape)


def whole_image(odd, part, from_second, from_first, valid):
    first, second = from_first[:HMAX], from_second[:HMAX]
    north_first = odd[1:2, :] == 1
    around = jnp.concatenate(
        [jnp.where(north_first, first, second), jnp.where(north_first, second, first)], axis=0
    )
    maskf = valid[...].astype(jnp.float32)
    return part[...] + maskf * around, maskf


def finish_kernel(step, odd, part, from_second, from_first, valid, *refs):
    out, second, first = refs[-5:-2] if step == 1 else refs
    image, maskf = whole_image(odd, part, from_second, from_first, valid)
    out[...] = image
    first[...], second[...] = edge_tiles(by_partner(maskf * image, odd), odd)
    if step == 1:
        to_second, to_first, masks_second, masks_first = refs[:4]
        q_second, q_first = refs[-2:]
        mask = masks_second[HMAX:]
        q_second[...] = mask * (from_second[HMAX:] + mask * to_second[:HMAX])
        mask = masks_first[HMAX:]
        q_first[...] = mask * (from_first[HMAX:] + mask * to_first[:HMAX])


def sum_kernel(parts, out):
    out[...] = jnp.broadcast_to(jnp.sum(parts[...], axis=0, keepdims=True), out.shape)


def solve_kernel(odd, parts, v0, v1, v2, part, from_second, from_first, valid, weights, residual):
    sums = jnp.sum(parts[...], axis=0)
    lane = lanes(sums.shape)
    gram = {}
    for k, (i, j) in enumerate(GRAM + [(2, 3)]):
        value = jnp.sum(jnp.where(lane == k, sums, 0.0), keepdims=True)
        gram[i, j] = gram[j, i] = value
    gram[0, 3], gram[1, 3] = gram[1, 2], gram[2, 2]

    def inner(a, b):
        total = None
        for i, x in a.items():
            for j, y in b.items():
                term = x * y * gram[i, j]
                total = term if total is None else total + term
        return total

    def combine(a, scale, b):
        out = dict(a)
        for i, y in b.items():
            out[i] = out[i] + scale * y if i in out else scale * y
        return out

    one = jnp.ones((1, 1), jnp.float32)
    w, r, d = {}, {0: one}, {0: one}
    now = inner(r, r)
    for step in range(3):
        image = {i + 1: x for i, x in d.items()}
        alpha = now / inner(d, image)
        w = combine(w, alpha, d)
        r = combine(r, -alpha, image)
        if step < 2:
            later = inner(r, r)
            d = combine(r, later / now, d)
            now = later
    basis = [v0[...], v1[...], v2[...], whole_image(odd, part, from_second, from_first, valid)[0]]
    weights[...] = w[0] * basis[0] + w[1] * basis[1] + w[2] * basis[2]
    residual[...] = r[0] * basis[0] + r[1] * basis[1] + r[2] * basis[2] + r[3] * basis[3]


def call(kernel, outs, *args, name=None, flops=0, **more):
    return pl.pallas_call(
        kernel,
        out_shape=outs,
        compiler_params=pltpu.CompilerParams(vmem_limit_bytes=VMEM_LIMIT),
        cost_estimate=pl.CostEstimate(
            flops=flops, transcendentals=0, bytes_accessed=sum(a.size * a.dtype.itemsize for a in args)
        ),
        name=name or kernel.__name__,
        **more,
    )(*args)


def shards(ensemble, right_side, obs_error, valid, halfwidth):
    members, rows, cols = ensemble.shape
    quads, planes = members // 4, members // 2
    bf16 = functools.partial(jax.ShapeDtypeStruct, dtype=jnp.bfloat16)
    f32 = functools.partial(jax.ShapeDtypeStruct, dtype=jnp.float32)
    odd_lon, odd_lat = lax.axis_index(LON) % 2, lax.axis_index("lat") % 2
    odd = jnp.where(jnp.arange(8)[:, None] == 0, odd_lon, odd_lat)
    odd = jnp.broadcast_to(odd, (8, cols)).astype(jnp.int32)
    lon_band, side_band = lon_bands(halfwidth[0], cols, odd_lon)
    lat = lat_band(halfwidth[1], rows, odd_lat)
    plain = pl.BlockSpec(memory_space=pltpu.VMEM)

    def with_odd(kernel, outs, *args, **more):
        return call(kernel, outs, odd, *args, in_specs=[plain] * (1 + len(args)), **more)

    q = valid.astype(jnp.float32) * right_side
    halves = with_odd(rows_kernel, [bf16((members, HMAX, cols))] * 2, ensemble)
    rows_second = swap(halves[0], "lat", 1, False)
    rows_first = swap(halves[1], "lat", 0, False)
    second, first = with_odd(
        columns_kernel, [bf16((quads + 2, rows, cols))] * 2, q, *halves
    )
    sides, q_sides = call(
        sides_kernel, [bf16((planes, rows, cols)), f32((rows, cols))],
        swap(second, LON, 1, True), swap(first, LON, 0, True),
    )
    around = [q_sides]
    vectors, more = [right_side], []
    flops = 8 * members * rows * cols * (cols + rows)
    for step in range(3):
        vector = vectors[-1]
        message = f32((2 * HMAX if step < 2 else HMAX, cols))
        part, to_second, to_first = with_odd(
            functools.partial(taper_kernel, step), [f32((rows, cols)), message, message],
            vector, valid, obs_error, *around, *halves, sides, rows_second, rows_first,
            lon_band, side_band, lat, name=f"taper_{step}", flops=flops,
        )
        from_second = swap(to_second, "lat", 1, False)
        from_first = swap(to_first, "lat", 0, False)
        if step == 2:
            break
        outs = [f32((rows, cols))] * 3
        if step == 1:
            outs += [f32((HMAX, cols))] * 2
            more = [to_second, to_first] + masks
        image, second, first, *more = with_odd(
            functools.partial(finish_kernel, step), outs, part, from_second, from_first, valid,
            *more, name=f"finish_{step}",
        )
        masks = [from_second, from_first]
        vectors.append(image)
        around = [swap(second, LON, 1, True), swap(first, LON, 0, True)]
    gram = call(
        gram_kernel, f32((lax.axis_size("far") * lax.axis_size("lat"), 1, 128)),
        *vectors, part, to_second, to_first, *more,
    )
    parts = lax.all_to_all(gram, ("far", "lat"), 0, 0)
    parts = call(sum_kernel, f32((lax.axis_size("near"), 1, 128)), parts)
    parts = lax.all_to_all(parts, "near", 0, 0)
    return tuple(
        with_odd(
            solve_kernel, [f32((rows, cols))] * 2, parts, *vectors, part, from_second,
            from_first, valid,
        )
    )


def solution(mesh):
    devices = mesh.devices
    parts = 2 if devices.shape[0] % 2 == 0 else 1
    mesh = Mesh(
        devices.reshape(parts, devices.shape[0] // parts, devices.shape[1]), LON + ("lat",)
    )
    in_specs = (P(None, "lat", LON), P("lat", LON), P("lat", LON), P("lat", LON), P())
    out_specs = (P("lat", LON), P("lat", LON))
    return jax.shard_map(shards, mesh=mesh, in_specs=in_specs, out_specs=out_specs, check_vma=False)
```
